32 devices in a mesh: segment: 4 (over y, x), dp: 8 (over z, core).
Axes of the slice: x: 2, y: 2, z: 4, core: 2. Of those that a mesh axis runs over, the one named last changes fastest.
Arguments:
- activations: bfloat16 [4, 64, 4, 4, 8, 256], P('segment', 'dp'), may hold values from -6 to 6
- preacts: bfloat16 [4, 64, 4, 4, 8, 256], P('segment', 'dp'), may hold values from -10 to 10
- out_grad: bfloat16 [64, 4, 4, 8, 256], P('dp'), may hold values from -6 to 6
- weights: float32 [4, 256, 27, 256], P('segment', 'dp'), may hold values from -0.078125 to 0.078125
- momentum: float32 [4, 256, 27, 256], P('segment', 'dp'), may hold values from -6 to 6
- noise: float32 [4, 256, 27, 256], P('segment', 'dp'), may hold values from -6 to 6
Outputs:
- new_momentum: float32 [4, 256, 27, 256], P('segment', 'dp')
The draws below stay inside these ranges and needn't reach their ends.
All inputs are finite; a program needn't handle non-finite values.
Results may differ from the reference program's by a relative error of at most 0.0033.
Values may be sent and summed in bfloat16 or wider, within the bound.
No kernel may reach another device: no remote copies, remote signals or barrier semaphores. Data moves between devices by JAX's collectives and lax.ppermute only.
A program may use at most 192 MiB of HBM per device.

```python
import math
import jax
import jax.numpy as jnp
from jax import lax

C = 256
TAPS = 27
CT = 4
CX = 4
CY = 8
MICRO = 8
CELLS = 128
SAMP = 64
SEGMENTS = 4
N_DP = 8


def steps_of(stream_key, shape, cuts, least, largest):
    def one(dim, shards_of):
        heights = jax.random.uniform(jax.random.fold_in(jax.random.fold_in(stream_key, 6), dim), (shards_of,), jnp.float32, least / len(cuts), largest / len(cuts))
        return jnp.repeat(jnp.exp(heights), shape[dim] // shards_of).reshape((-1,) + (1,) * (len(shape) - dim - 1))

    loudness = one(*cuts[0])
    for cut in cuts[1:]:
        loudness = loudness * one(*cut)
    return loudness


def bell_draw(own_key, shape, scale, bound, shards=(), kind=jnp.bfloat16):
    factor_of = steps_of(own_key, shape, shards, -0.22, 0.18) if shards else 1.0
    drawn = jax.random.normal(own_key, shape, jnp.float32) * scale * factor_of
    return jnp.minimum(jnp.maximum(drawn, -bound), bound).astype(kind)


def setup_inputs(seed: int = 0) -> dict:
    key_of = jax.random.split(jax.random.key(seed), 7)
    return {
        "activations": bell_draw(key_of[0], (SEGMENTS, SAMP, CT, CX, CY, C), 1.0, 6.0, ((0, 4), (1, 8))),
        "preacts": bell_draw(key_of[1], (SEGMENTS, SAMP, CT, CX, CY, C), 2.0, 10.0, ((0, 4), (1, 8))),
        "out_grad": bell_draw(key_of[2], (SAMP, CT, CX, CY, C), 1.0, 6.0, ((0, 8),)),
        "weights": bell_draw(key_of[3], (SEGMENTS, C, TAPS, C), (C * TAPS) ** -0.5, 0.078125, ((0, 4), (1, 8)), jnp.float32),
        "momentum": bell_draw(key_of[4], (SEGMENTS, C, TAPS, C), 1.0, 6.0, ((0, 4), (1, 8)), jnp.float32),
        "noise": bell_draw(key_of[5], (SEGMENTS, C, TAPS, C), 1.0, 6.0, ((0, 4), (1, 8)), jnp.float32),
    }


def tap_stack(field, sign):
    batch_n, span_t, span_x, span_y, channels = field.shape
    padded = jnp.pad(field, ((0, 0), (1, 1), (1, 1), (1, 1), (0, 0)))
    views = []
    for along_t in (-1, 0, 1):
        for along_x in (-1, 0, 1):
            for along_y in (-1, 0, 1):
                start_t = 1 + sign * along_t
                start_x = 1 + sign * along_x
                start_y = 1 + sign * along_y
                views.append(padded[:, start_t:start_t + span_t, start_x:start_x + span_x, start_y:start_y + span_y, :])
    return jnp.stack(views, axis=4).reshape(batch_n * span_t * span_x * span_y, 27, channels)

def reference(activations, preacts, out_grad, weights, momentum, noise):
    segments = activations.shape[0]
    crop_shape = activations.shape[2:]
    grads = []
    upstream_all = out_grad
    for segment in range(segments - 1, -1, -1):
        rounded = lax.optimization_barrier(weights[segment].astype(jnp.bfloat16))
        kernel = rounded.astype(jnp.float32)
        group_in = activations[segment].reshape((N_DP, MICRO) + crop_shape)
        group_pre = preacts[segment].reshape((N_DP, MICRO) + crop_shape)
        group_up = upstream_all.reshape((N_DP, MICRO) + crop_shape)

        def group_step(total, pieces):
            inputs, pres, upstream = pieces
            pre = pres.astype(jnp.float32)
            sig = jax.nn.sigmoid(pre)
            up_wide = upstream.astype(jnp.float32)
            grad_pre = (up_wide * sig * (1.0 + pre * (1.0 - sig))).astype(jnp.bfloat16)
            pre_cols = tap_stack(grad_pre, -1).astype(jnp.float32)
            back = jnp.einsum('nto,cto->nc', pre_cols, kernel)
            passed = (up_wide + back.reshape(upstream.shape)).astype(jnp.bfloat16)
            in_cols = tap_stack(inputs, 1).astype(jnp.float32)
            flat_pre = grad_pre.reshape(-1, C).astype(jnp.float32)
            total = total + jnp.einsum('ntc,no->cto', in_cols, flat_pre)
            return (total, passed)
        total, passed = lax.scan(group_step, jnp.zeros((C, TAPS, C), jnp.float32), (group_in, group_pre, group_up))
        grads.append(total)
        upstream_all = passed.reshape(out_grad.shape)
    grads = jnp.stack(grads[::-1])
    rate = 1.0 / math.sqrt(SAMP * CELLS)
    return 0.9 * momentum - rate * grads + 0.3 * noise
```

```python
import functools
import math

import jax
import jax.numpy as jnp
from jax import lax
from jax.experimental import pallas as pl
from jax.experimental.pallas import tpu as pltpu
from jax.sharding import PartitionSpec as P

BF16 = jnp.bfloat16
F32 = jnp.float32
VMEM_BYTES = 48 * 1024 * 1024


def shifted(x, axis, by):
    size = lax.axis_size(axis)
    pairs = [(i, i + by) for i in range(size) if 0 <= i + by < size]
    return lax.ppermute(x, axis, pairs)


def swapped(x, axis, mask):
    return lax.ppermute(x, axis, [(i, i ^ mask) for i in range(lax.axis_size(axis))])


def tap_stack(field, sign):
    batch_n, span_t, span_x, span_y, channels = field.shape
    padded = jnp.pad(field, ((0, 0), (1, 1), (1, 1), (1, 1), (0, 0)))
    views = []
    for along_t in (-1, 0, 1):
        for along_x in (-1, 0, 1):
            for along_y in (-1, 0, 1):
                start_t = 1 + sign * along_t
                start_x = 1 + sign * along_x
                start_y = 1 + sign * along_y
                views.append(
                    padded[
                        :,
                        start_t : start_t + span_t,
                        start_x : start_x + span_x,
                        start_y : start_y + span_y,
                        :,
                    ]
                )
    return jnp.stack(views, axis=4).reshape(batch_n * span_t * span_x * span_y, 27, channels)


def general_shards(activations, preacts, out_grad, weights, momentum, noise):
    segments = lax.axis_size("segment")
    devices_dp = lax.axis_size("dp")
    segment_id = lax.axis_index("segment")
    kernel = lax.all_gather(weights.astype(BF16), "dp", axis=1, tiled=True)[0]
    inputs = activations[0]
    pres = preacts[0]
    micro, span_t, span_x, span_y, channels = inputs.shape
    cells = span_t * span_x * span_y
    is_last = segment_id == segments - 1

    def step_fn(step, carry):
        incoming, total = carry
        index = step - (segments - 1 - segment_id)
        valid = jnp.logical_and(index >= 0, index < micro)
        clipped = jnp.clip(index, 0, micro - 1)
        given = lax.dynamic_index_in_dim(out_grad, clipped, 0, keepdims=False)
        upstream = jnp.where(is_last, given, incoming)
        pre = lax.dynamic_index_in_dim(pres, clipped, 0, keepdims=False).astype(F32)
        sig = jax.nn.sigmoid(pre)
        up_wide = upstream.astype(F32)
        grad_pre = (up_wide * sig * (1.0 + pre * (1.0 - sig)) * valid.astype(F32)).astype(BF16)
        pre_cols = tap_stack(grad_pre[None], -1)
        back = jnp.einsum("nto,cto->nc", pre_cols, kernel, preferred_element_type=F32)
        passed = (up_wide + back.reshape(upstream.shape)).astype(BF16)
        in_cols = tap_stack(lax.dynamic_index_in_dim(inputs, clipped, 0, keepdims=True), 1)
        total = total + jnp.einsum(
            "ntc,no->cto", in_cols, grad_pre.reshape(cells, channels), preferred_element_type=F32
        )
        return shifted(passed, "segment", -1), total

    init = (jnp.zeros(inputs.shape[1:], BF16), jnp.zeros((channels, 27, channels), F32))
    total = lax.fori_loop(0, micro + segments - 1, step_fn, init)[1]
    owned = lax.psum_scatter(total, "dp", scatter_dimension=0, tiled=True)
    rate = 1.0 / math.sqrt(devices_dp * micro * cells)
    return (0.9 * momentum[0] - rate * owned + 0.3 * noise[0])[None]


def iota(shape, dim):
    return lax.broadcasted_iota(jnp.int32, shape, dim)


def log2(n):
    return n.bit_length() - 1


def channel_of(place, quarter, per, sub):
    return (place >> log2(sub)) * per + quarter * sub + (place & (sub - 1))


def dot(a, b):
    return jnp.dot(a, b, preferred_element_type=F32)


def call(body, out_shape, args, flops=0, scratch=()):
    bytes_accessed = sum(x.size * x.dtype.itemsize for x in args)
    return pl.pallas_call(
        body,
        out_shape=out_shape,
        in_specs=[pl.BlockSpec(memory_space=pltpu.SMEM)]
        + [pl.BlockSpec(memory_space=pltpu.VMEM)] * (len(args) - 1),
        out_specs=jax.tree.map(lambda _: pl.BlockSpec(memory_space=pltpu.VMEM), out_shape),
        scratch_shapes=list(scratch),
        compiler_params=pltpu.CompilerParams(vmem_limit_bytes=VMEM_BYTES),
        cost_estimate=pl.CostEstimate(
            flops=flops, bytes_accessed=bytes_accessed, transcendentals=0
        ),
    )(*args)


def weights_body(per, sub, ids, w_ref, *out_refs):
    channels = w_ref.shape[2]
    quarter_n = channels // 4
    s = ids[0]
    for m, out_ref in enumerate(out_refs):
        target = s ^ m
        rows = [
            w_ref[pl.ds(target * sub, sub), t, :] for t in range(27)
        ]
        stacked = jnp.concatenate(rows, axis=0).astype(BF16)
        lane = iota((channels, channels), 1)
        place = lane & (quarter_n - 1)
        quarter = (lane >> log2(quarter_n)) ^ target
        order = iota((channels, channels), 0) == channel_of(place, quarter, per, sub)
        moved = dot(stacked, order.astype(BF16))
        for bc in range(9):
            part = [moved[(a * 9 + bc) * sub : (a * 9 + bc + 1) * sub] for a in range(3)]
            out_ref[:, bc * channels : (bc + 1) * channels] = jnp.concatenate(part, axis=0).astype(
                BF16
            )


def quarters_body(per, sub, ids, pre_ref, up_ref, up_out, *out_refs):
    rows, channels = pre_ref.shape
    quarter_n = channels // 4
    half = rows // 2
    s = ids[0]
    shape = (channels, 8 * quarter_n)
    lane = iota(shape, 1)
    place = lane & (quarter_n - 1)
    quarter = (lane >> log2(2 * quarter_n)) ^ s
    hit = iota(shape, 0) == channel_of(place, quarter, per, sub)
    low = (lane & (2 * quarter_n - 1)) < quarter_n
    first = jnp.logical_and(hit, low).astype(BF16)
    second = jnp.logical_and(hit, jnp.logical_not(low)).astype(BF16)
    packed = dot(pre_ref[:half], first) + dot(pre_ref[half:], second)
    for m, out_ref in enumerate(out_refs):
        out_ref[...] = packed[:, m * 2 * quarter_n : (m + 1) * 2 * quarter_n].astype(BF16)
    width = 2 * quarter_n
    up_out[...] = (dot(up_ref[:half], first[:, :width]) + dot(up_ref[half:], second[:, :width])).astype(BF16)


def silu_back(up_wide, pre):
    pre = pre.astype(F32)
    sig = jax.nn.sigmoid(pre)
    return (up_wide * sig * (1.0 + pre * (1.0 - sig))).astype(BF16)


def shifts(field, span):
    span_x, span_y = span
    rows, lanes = field.shape
    y = iota((rows, lanes), 0) & (span_y - 1)
    along_y = (
        jnp.where(y == span_y - 1, 0.0, pltpu.roll(field, rows - 1, 0)),
        field,
        jnp.where(y == 0, 0.0, pltpu.roll(field, 1, 0)),
    )
    out = []
    for b in (-1, 0, 1):
        for c in (-1, 0, 1):
            part = along_y[c + 1].reshape(rows // (span_x * span_y), span_x, span_y, lanes)
            edge = jnp.zeros_like(part[:, :1])
            if b == 1:
                part = jnp.concatenate([edge, part[:, :-1]], axis=1)
            elif b == -1:
                part = jnp.concatenate([part[:, 1:], edge], axis=1)
            out.append(part.reshape(rows, lanes))
    return out


def back_body(span, n_dp, ids, g0, g1, g2, g3, w_ref, up_ref, pre_ref, up_out, g_out, cols):
    span_t, span_x, span_y = span
    half, width = g0.shape
    quarter_n = width // 2
    channels = 4 * quarter_n
    sub = quarter_n // n_dp
    rows = 2 * half
    plane = span_x * span_y
    d = ids[1]
    shape = (4 * width, 2 * channels)
    src, dst = iota(shape, 0), iota(shape, 1)
    m, h, place = src >> log2(width), (src >> log2(quarter_n)) & 1, src & (quarter_n - 1)
    unpack = (dst == h * channels + m * quarter_n + place).astype(BF16)
    both = dot(jnp.concatenate([g0[...], g1[...], g2[...], g3[...]], axis=1), unpack)
    field = jnp.concatenate([both[:, :channels], both[:, channels:]], axis=0)
    for k, part in enumerate(shifts(field, (span_x, span_y))):
        cols[:, k * channels : (k + 1) * channels] = part.astype(BF16)
    shape = (3 * quarter_n, 3 * quarter_n)
    dst, src = iota(shape, 0), iota(shape, 1)
    a, place = dst >> log2(quarter_n), dst & (quarter_n - 1)
    apart = (place >> log2(sub)) ^ d
    piece = (apart >> 1) + (n_dp // 2) * (apart & 1)
    order = src == piece * (3 * sub) + a * sub + (place & (sub - 1))
    kernel = dot(order.astype(BF16), w_ref[...]).astype(BF16)
    terms = lax.dot_general(
        cols[...], kernel, (((1,), (1,)), ((), ())), preferred_element_type=F32
    )
    back = []
    for a in range(3):
        back.append(
            terms[:, a * quarter_n : (a + 1) * quarter_n].reshape(
                rows // (span_t * plane), span_t, plane, quarter_n
            )
        )
    edge = jnp.zeros_like(back[0][:, :1])
    total = (
        back[1]
        + jnp.concatenate([back[0][:, 1:], edge], axis=1)
        + jnp.concatenate([edge, back[2][:, :-1]], axis=1)
    ).reshape(rows, quarter_n)
    total = jnp.concatenate([total[:half], total[half:]], axis=1)
    passed = (up_ref[...].astype(F32) + total).astype(BF16)
    up_out[...] = passed
    g_out[...] = silu_back(passed.astype(F32), pre_ref[...])


def grads_body(span, n_dp, ids, g_ref, x_ref, keep, give, cols, total):
    span_t, span_x, span_y = span
    half, width = g_ref.shape
    quarter_n = width // 2
    rows, channels = x_ref.shape
    per = channels // n_dp
    plane = span_x * span_y
    crops = rows // (span_t * plane)
    d = ids[1]
    shape = (width, 2 * width)
    src, dst = iota(shape, 0), iota(shape, 1)
    twice = jnp.logical_and(
        (src & (quarter_n - 1)) == (dst & (quarter_n - 1)),
        (src >> log2(quarter_n)) == (dst >> log2(width)),
    ).astype(BF16)
    both = dot(g_ref[...], twice)
    field = jnp.concatenate([both[:, :width], both[:, width:]], axis=0)
    parts = shifts(field, (span_x, span_y))
    left = iota((rows, width), 1) < quarter_n
    for k in range(5):
        other = parts[2 * k + 1] if k < 4 else 0.0
        cols[:, k * width : (k + 1) * width] = jnp.where(left, parts[2 * k], other).astype(BF16)
    inputs = x_ref[...].reshape(crops, span_t, plane, channels)
    taken = cols[...].reshape(crops, span_t, plane, 5 * width)
    for a in (-1, 0, 1):
        x_a = inputs[:, max(a, 0) : span_t + min(a, 0)].reshape(-1, channels)
        g_a = taken[:, max(-a, 0) : span_t + min(-a, 0)].reshape(-1, 5 * width)
        total[(a + 1) * channels : (a + 2) * channels, :] = lax.dot_general(
            x_a, g_a, (((0,), (0,)), ((), ())), preferred_element_type=F32
        )
    for k in range(n_dp // 2):
        for bit, ref in ((0, keep), (1, give)):
            owner = d ^ (2 * k + bit)
            for a in range(3):
                ref[k, a * per : (a + 1) * per, :] = total[
                    pl.ds(pl.multiple_of(a * channels + owner * per, per), per), :
                ].astype(ref.dtype)


def pair_body(ids, keep, other, own, *out_refs):
    own[...] = keep[0] + other[0].astype(F32)
    for k, out_ref in enumerate(out_refs):
        out_ref[...] = (keep[k + 1] + other[k + 1].astype(F32)).astype(BF16)


def sums_body(pieces, ids, *refs):
    ins, outs = refs[: 4 * pieces], refs[4 * pieces :]
    s = ids[0]
    for section in range(4):
        parts = ins[section * pieces : (section + 1) * pieces]
        total = parts[0][...]
        for part in parts[1:]:
            total = total + part[...].astype(F32)
        for m, out_ref in enumerate(outs):
            @pl.when((s ^ m) == section)
            def _(out_ref=out_ref, total=total):
                out_ref[...] = total.astype(BF16)


def update_body(per, sub, rate, ids, f0, f1, f2, f3, momentum, noise, out):
    channels = momentum.shape[2]
    quarter_n = channels // 4
    width = 2 * quarter_n
    s = ids[0]
    shape = (4 * width, 2 * channels)
    src, dst = iota(shape, 0), iota(shape, 1)
    m, h, place = src >> log2(width), (src >> log2(quarter_n)) & 1, src & (quarter_n - 1)
    order = (dst == h * channels + channel_of(place, m ^ s, per, sub)).astype(BF16)
    for k in range(5):
        lanes = slice(k * width, (k + 1) * width)
        grads = dot(jnp.concatenate([f[:, lanes] for f in (f0, f1, f2, f3)], axis=1), order)
        for h in range(2 if k < 4 else 1):
            for a in range(3):
                t = a * 9 + 2 * k + h
                own = grads[a * per : (a + 1) * per, h * channels : (h + 1) * channels]
                out[:, t, :] = 0.9 * momentum[:, t, :] - rate * own + 0.3 * noise[:, t, :]


def pick(index, arrays):
    return lax.select_n(index, *arrays)


def quartered_shards(activations, preacts, out_grad, weights, momentum, noise):
    n_dp = lax.axis_size("dp")
    s = lax.axis_index("segment").astype(jnp.int32)
    d = lax.axis_index("dp").astype(jnp.int32)
    ids = jnp.stack([s, d])
    micro, span_t, span_x, span_y, channels = out_grad.shape
    span = (span_t, span_x, span_y)
    rows = micro * span_t * span_x * span_y
    quarter_n = channels // 4
    width = 2 * quarter_n
    half = rows // 2
    per = channels // n_dp
    sub = per // 4
    chips = n_dp // 2
    inputs = activations.reshape(rows, channels)
    pres = preacts.reshape(rows, channels)
    packed = jax.ShapeDtypeStruct((half, width), BF16)
    taken = 5 * width

    w_parts = call(
        functools.partial(weights_body, per, sub),
        [jax.ShapeDtypeStruct((3 * sub, 9 * channels), BF16)] * 4,
        (ids, weights[0]),
    )
    w_held = [w_parts[0]] + [swapped(w_parts[m], "segment", m) for m in (3, 1, 2)]
    w_held = [w_held[0], w_held[2], w_held[3], w_held[1]]
    up, *p_parts = call(
        functools.partial(quarters_body, per, sub),
        [packed] * 5,
        (ids, pres, out_grad.reshape(rows, channels)),
    )
    p_held = [p_parts[0]] + [swapped(p_parts[m], "segment", m) for m in (3, 1, 2)]
    p_held = [p_held[0], p_held[2], p_held[3], p_held[1]]

    def gathered(section):
        own = pick(s ^ section, w_held)
        pieces = jnp.stack([own] + [swapped(own, "dp", 2 * k) for k in range(1, chips)])
        other = swapped(pieces, "dp", 1)
        return jnp.concatenate([pieces, other], axis=0).reshape(3 * quarter_n, 9 * channels)

    def spread(x):
        far, one, two = (swapped(x, "segment", m) for m in (3, 1, 2))
        return x, one, two, far

    def reduced(section, g):
        keep, give = call(
            functools.partial(grads_body, span, n_dp),
            [
                jax.ShapeDtypeStruct((chips, 3 * per, taken), F32),
                jax.ShapeDtypeStruct((chips, 3 * per, taken), BF16),
            ],
            (ids, g, pick(s ^ section, x_held)),
            scratch=[pltpu.VMEM((rows, taken), BF16), pltpu.VMEM((3 * channels, taken), F32)],
        )
        own, *out = call(
            pair_body,
            [jax.ShapeDtypeStruct((3 * per, taken), F32)]
            + [jax.ShapeDtypeStruct((3 * per, taken), BF16)] * (chips - 1),
            (ids, keep, swapped(give, "dp", 1)),
        )
        return [own] + [swapped(x, "dp", 2 * (k + 1)) for k, x in enumerate(out)]

    kernels = {3: gathered(3)}
    g = silu_back(up.astype(F32), pick(s ^ 3, p_held))
    fields = {3: spread(g)}
    x_held = spread(inputs)
    kernels[2] = gathered(2)
    kernels[1] = gathered(1)
    sums = {}
    for section in (3, 2, 1):
        up, g = call(
            functools.partial(back_body, span, n_dp),
            [packed] * 2,
            (ids, *fields[section], kernels[section], up, pick(s ^ (section - 1), p_held)),
            scratch=[pltpu.VMEM((rows, 9 * channels), BF16)],
        )
        fields[section - 1] = spread(g) if section > 1 else (g,)
        sums[section] = reduced(section, fields[section][0])
    sums[0] = reduced(0, g)
    owned = call(
        functools.partial(sums_body, chips),
        [jax.ShapeDtypeStruct((3 * per, taken), BF16)] * 4,
        (ids, *sums[0], *sums[1], *sums[2], *sums[3]),
    )
    far, one, two = (swapped(owned[m], "segment", m) for m in (3, 1, 2))
    rate = 1.0 / math.sqrt(n_dp * rows)
    return call(
        functools.partial(update_body, per, sub, rate),
        jax.ShapeDtypeStruct(momentum.shape[1:], F32),
        (ids, owned[0], one, two, far, momentum[0], noise[0]),
    )[None]


def solution(mesh):
    placed = (
        P("segment", "dp", None, None, None, None),
        P("segment", "dp", None, None, None, None),
        P("dp", None, None, None, None),
        P("segment", "dp", None, None),
        P("segment", "dp", None, None),
        P("segment", "dp", None, None),
    )

    def shards(activations, preacts, out_grad, weights, momentum, noise):
        channels = weights.shape[-1]
        n_dp = mesh.shape["dp"]
        fits = (
            mesh.shape["segment"] == 4
            and channels % (32 * n_dp) == 0
            and n_dp & (n_dp - 1) == 0
            and out_grad.shape[3] == 8
        )
        plan = quartered_shards if fits else general_shards
        return plan(activations, preacts, out_grad, weights, momentum, noise)

    return jax.shard_map(
        shards,
        mesh=mesh,
        in_specs=placed,
        out_specs=P("segment", "dp", None, None),
        check_vma=False,
    )
```

```python
import functools
import math

import jax
import jax.numpy as jnp
from jax import lax
from jax.experimental import pallas as pl
from jax.experimental.pallas import tpu as pltpu
from jax.sharding import PartitionSpec as P

BF16 = jnp.bfloat16
F32 = jnp.float32
VMEM_BYTES = 48 * 1024 * 1024
PEAK_PER_US = 1.1535e9


def shifted(x, axis, by):
    size = lax.axis_size(axis)
    pairs = [(i, i + by) for i in range(size) if 0 <= i + by < size]
    return lax.ppermute(x, axis, pairs)


def swapped(x, axis, mask):
    return lax.ppermute(x, axis, [(i, i ^ mask) for i in range(lax.axis_size(axis))])


def tap_stack(field, sign):
    batch_n, span_t, span_x, span_y, channels = field.shape
    padded = jnp.pad(field, ((0, 0), (1, 1), (1, 1), (1, 1), (0, 0)))
    views = []
    for along_t in (-1, 0, 1):
        for along_x in (-1, 0, 1):
            for along_y in (-1, 0, 1):
                start_t = 1 + sign * along_t
                start_x = 1 + sign * along_x
                start_y = 1 + sign * along_y
                views.append(
                    padded[
                        :,
                        start_t : start_t + span_t,
                        start_x : start_x + span_x,
                        start_y : start_y + span_y,
                        :,
                    ]
                )
    return jnp.stack(views, axis=4).reshape(batch_n * span_t * span_x * span_y, 27, channels)


def general_shards(activations, preacts, out_grad, weights, momentum, noise):
    segments = lax.axis_size("segment")
    devices_dp = lax.axis_size("dp")
    segment_id = lax.axis_index("segment")
    kernel = lax.all_gather(weights.astype(BF16), "dp", axis=1, tiled=True)[0]
    inputs = activations[0]
    pres = preacts[0]
    micro, span_t, span_x, span_y, channels = inputs.shape
    cells = span_t * span_x * span_y
    is_last = segment_id == segments - 1

    def step_fn(step, carry):
        incoming, total = carry
        index = step - (segments - 1 - segment_id)
        valid = jnp.logical_and(index >= 0, index < micro)
        clipped = jnp.clip(index, 0, micro - 1)
        given = lax.dynamic_index_in_dim(out_grad, clipped, 0, keepdims=False)
        upstream = jnp.where(is_last, given, incoming)
        pre = lax.dynamic_index_in_dim(pres, clipped, 0, keepdims=False).astype(F32)
        sig = jax.nn.sigmoid(pre)
        up_wide = upstream.astype(F32)
        grad_pre = (up_wide * sig * (1.0 + pre * (1.0 - sig)) * valid.astype(F32)).astype(BF16)
        pre_cols = tap_stack(grad_pre[None], -1)
        back = jnp.einsum("nto,cto->nc", pre_cols, kernel, preferred_element_type=F32)
        passed = (up_wide + back.reshape(upstream.shape)).astype(BF16)
        in_cols = tap_stack(lax.dynamic_index_in_dim(inputs, clipped, 0, keepdims=True), 1)
        total = total + jnp.einsum(
            "ntc,no->cto", in_cols, grad_pre.reshape(cells, channels), preferred_element_type=F32
        )
        return shifted(passed, "segment", -1), total

    init = (jnp.zeros(inputs.shape[1:], BF16), jnp.zeros((channels, 27, channels), F32))
    total = lax.fori_loop(0, micro + segments - 1, step_fn, init)[1]
    owned = lax.psum_scatter(total, "dp", scatter_dimension=0, tiled=True)
    rate = 1.0 / math.sqrt(devices_dp * micro * cells)
    return (0.9 * momentum[0] - rate * owned + 0.3 * noise[0])[None]


def iota(shape, dim):
    return lax.broadcasted_iota(jnp.int32, shape, dim)


def log2(n):
    return n.bit_length() - 1


def channel_of(place, quarter, per, sub):
    return (place >> log2(sub)) * per + quarter * sub + (place & (sub - 1))


def dot(a, b):
    return jnp.dot(a, b, preferred_element_type=F32)


def call(body, out_shape, args, us, scratch=()):
    return pl.pallas_call(
        body,
        out_shape=out_shape,
        in_specs=[pl.BlockSpec(memory_space=pltpu.SMEM)]
        + [pl.BlockSpec(memory_space=pltpu.VMEM)] * (len(args) - 1),
        out_specs=jax.tree.map(lambda _: pl.BlockSpec(memory_space=pltpu.VMEM), out_shape),
        scratch_shapes=list(scratch),
        compiler_params=pltpu.CompilerParams(vmem_limit_bytes=VMEM_BYTES),
        cost_estimate=pl.CostEstimate(
            flops=int(us * PEAK_PER_US), bytes_accessed=0, transcendentals=0
        ),
    )(*args)


def weights_body(per, sub, ids, w_ref, *out_refs):
    channels = w_ref.shape[2]
    quarter_n = channels // 4
    s = ids[0]
    lane = iota((channels, channels), 1)
    place = lane & (quarter_n - 1)
    for m, out_ref in enumerate(out_refs):
        target = s ^ m
        own = w_ref[:, pl.ds(pl.multiple_of(target * sub, sub), sub), :]
        quarter = (lane >> log2(quarter_n)) ^ target
        order = iota((channels, channels), 0) == channel_of(place, quarter, per, sub)
        moved = dot(own.reshape(27 * sub, channels).astype(BF16), order.astype(BF16))
        for bc in range(9):
            part = [moved[(a * 9 + bc) * sub : (a * 9 + bc + 1) * sub] for a in range(3)]
            out_ref[:, bc * channels : (bc + 1) * channels] = jnp.concatenate(part, axis=0).astype(
                BF16
            )


def packing(channels, s, per, sub):
    quarter_n = channels // 4
    shape = (channels, 8 * quarter_n)
    lane = iota(shape, 1)
    place = lane & (quarter_n - 1)
    quarter = (lane >> log2(2 * quarter_n)) ^ s
    hit = iota(shape, 0) == channel_of(place, quarter, per, sub)
    low = (lane & (2 * quarter_n - 1)) < quarter_n
    first = jnp.logical_and(hit, low).astype(BF16)
    second = jnp.logical_and(hit, jnp.logical_not(low)).astype(BF16)
    return first, second


def packed_into(refs, field, first, second):
    half = field.shape[0] // 2
    width = first.shape[1] // 4
    lanes = width * len(refs)
    moved = dot(field[:half], first[:, :lanes]) + dot(field[half:], second[:, :lanes])
    for m, ref in enumerate(refs):
        ref[...] = moved[:, m * width : (m + 1) * width].astype(BF16)


def preacts_body(per, sub, ids, pre_ref, up_ref, up_out, *out_refs):
    first, second = packing(pre_ref.shape[1], ids[0], per, sub)
    packed_into(out_refs, pre_ref, first, second)
    packed_into([up_out], up_ref, first, second)


def first_body(per, sub, ids, up_ref, pre_ref, x_ref, *out_refs):
    half = up_ref.shape[0]
    packed_into([r.at[half:] for r in out_refs], x_ref, *packing(x_ref.shape[1], ids[0], per, sub))
    grad_pre = silu_back(up_ref[...].astype(F32), pre_ref[...])
    for ref in out_refs:
        ref[:half] = grad_pre


def silu_back(up_wide, pre):
    pre = pre.astype(F32)
    sig = jax.nn.sigmoid(pre)
    return (up_wide * sig * (1.0 + pre * (1.0 - sig))).astype(BF16)


def shifts(field, span):
    span_x, span_y = span
    rows, lanes = field.shape
    y = iota((rows, lanes), 0) & (span_y - 1)
    along_y = (
        jnp.where(y == span_y - 1, 0.0, pltpu.roll(field, rows - 1, 0)),
        field,
        jnp.where(y == 0, 0.0, pltpu.roll(field, 1, 0)),
    )
    out = []
    for b in (-1, 0, 1):
        for c in (-1, 0, 1):
            part = along_y[c + 1].reshape(rows // (span_x * span_y), span_x, span_y, lanes)
            edge = jnp.zeros_like(part[:, :1])
            if b == 1:
                part = jnp.concatenate([edge, part[:, :-1]], axis=1)
            elif b == -1:
                part = jnp.concatenate([part[:, 1:], edge], axis=1)
            out.append(part.reshape(rows, lanes))
    return out


def fill_columns(cols, parts, half, span):
    width = parts[0].shape[1]
    quarter_n = width // 2
    channels = 4 * quarter_n
    shape = (4 * width, 2 * channels)
    src, dst = iota(shape, 0), iota(shape, 1)
    m, h, place = src >> log2(width), (src >> log2(quarter_n)) & 1, src & (quarter_n - 1)
    unpack = (dst == h * channels + m * quarter_n + place).astype(BF16)
    both = dot(jnp.concatenate([part[:half] for part in parts], axis=1), unpack)
    field = jnp.concatenate([both[:, :channels], both[:, channels:]], axis=0)
    for k, part in enumerate(shifts(field, span[1:])):
        cols[:, k * channels : (k + 1) * channels] = part.astype(BF16)


def back_body(span, n_dp, ids, g0, g1, g2, g3, w_ref, up_ref, pre_ref, up_out, g_out, cols):
    span_t, span_x, span_y = span
    half, width = up_ref.shape
    quarter_n = width // 2
    sub = quarter_n // n_dp
    rows = 2 * half
    plane = span_x * span_y
    d = ids[1]
    fill_columns(cols, (g0, g1, g2, g3), half, span)
    shape = (3 * quarter_n, 3 * quarter_n)
    dst, src = iota(shape, 0), iota(shape, 1)
    a, place = dst >> log2(quarter_n), dst & (quarter_n - 1)
    apart = (place >> log2(sub)) ^ d
    piece = ((apart >> 2) & 1) + (apart & 2) + (n_dp // 2) * (apart & 1)
    order = src == piece * (3 * sub) + a * sub + (place & (sub - 1))
    kernel = dot(order.astype(BF16), w_ref[...]).astype(BF16)
    terms = lax.dot_general(
        cols[...], kernel, (((1,), (1,)), ((), ())), preferred_element_type=F32
    )
    back = []
    for a in range(3):
        back.append(
            terms[:, a * quarter_n : (a + 1) * quarter_n].reshape(
                rows // (span_t * plane), span_t, plane, quarter_n
            )
        )
    edge = jnp.zeros_like(back[0][:, :1])
    total = (
        back[1]
        + jnp.concatenate([back[0][:, 1:], edge], axis=1)
        + jnp.concatenate([edge, back[2][:, :-1]], axis=1)
    ).reshape(rows, quarter_n)
    total = jnp.concatenate([total[:half], total[half:]], axis=1)
    passed = (up_ref[...].astype(F32) + total).astype(BF16)
    up_out[...] = passed
    g_out[...] = silu_back(passed.astype(F32), pre_ref[...])


def grads_body(span, n_dp, ids, g0, g1, g2, g3, x_ref, keep, give, cols, total):
    span_t, span_x, span_y = span
    half, width = x_ref.shape
    quarter_n = width // 2
    sub = quarter_n // n_dp
    plane = span_x * span_y
    d = ids[1]
    fill_columns(cols, (g0, g1, g2, g3), half, span)
    shape = (width, 2 * width)
    src, dst = iota(shape, 0), iota(shape, 1)
    twice = jnp.logical_and(
        (src & (quarter_n - 1)) == (dst & (quarter_n - 1)),
        (src >> log2(quarter_n)) == (dst >> log2(width)),
    ).astype(BF16)
    both = dot(x_ref[...], twice)
    field = jnp.concatenate([both[:, :width], both[:, width:]], axis=0)
    field = field.reshape(2 * half // (span_t * plane), span_t, plane, width)
    edge = jnp.zeros_like(field[:, :1])
    later = jnp.concatenate([field[:, 1:], edge], axis=1)
    earlier = jnp.concatenate([edge, field[:, :-1]], axis=1)
    left = iota(field.shape, 3) < quarter_n
    taps = jnp.concatenate([jnp.where(left, earlier, field), later], axis=3)
    taps = taps.reshape(2 * half, 2 * width)[:, : 3 * quarter_n].astype(BF16)
    total[...] = lax.dot_general(
        taps, cols[...], (((0,), (0,)), ((), ())), preferred_element_type=F32
    )
    for k in range(n_dp // 2):
        for bit, ref in ((0, keep), (1, give)):
            owner = d ^ (2 * k + bit)
            own = [
                total[pl.ds(pl.multiple_of(a * quarter_n + owner * sub, sub), sub), :]
                for a in range(3)
            ]
            ref[k] = jnp.concatenate(own, axis=0).astype(ref.dtype)


def pair_body(ids, keep, other, stay, send):
    for k in range(keep.shape[0]):
        total = keep[k] + other[k].astype(F32)
        if k % 2 == 0:
            stay[k // 2] = total
        else:
            send[k // 2] = total.astype(BF16)


def next_body(ids, stay, other, own, send):
    own[...] = stay[0] + other[0].astype(F32)
    send[...] = (stay[1] + other[1].astype(F32)).astype(BF16)


def sums_body(ids, *refs):
    ins, outs = refs[:8], refs[8:]
    s = ids[0]
    for section in range(4):
        total = (ins[2 * section][...] + ins[2 * section + 1][...].astype(F32)).astype(BF16)
        for m, out_ref in enumerate(outs):
            @pl.when((s ^ m) == section)
            def _(out_ref=out_ref, total=total):
                out_ref[...] = total


def update_body(per, sub, rate, ids, f0, f1, f2, f3, momentum, noise, out):
    channels = momentum.shape[2]
    quarter_n = channels // 4
    s = ids[0]
    lane = iota((channels, channels), 0)
    for m, f in enumerate((f0, f1, f2, f3)):
        source = s ^ m
        place, quarter = lane & (quarter_n - 1), (lane >> log2(quarter_n)) ^ source
        order = iota((channels, channels), 1) == channel_of(place, quarter, per, sub)
        wide = f[...].astype(F32)
        parts = [
            wide[a * sub : (a + 1) * sub, bc * channels : (bc + 1) * channels]
            for a in range(3)
            for bc in range(9)
        ]
        grads = dot(jnp.concatenate(parts, axis=0).astype(BF16), order.astype(BF16))
        rows = pl.ds(pl.multiple_of(source * sub, sub), sub)
        out[:, rows, :] = (
            0.9 * momentum[:, rows, :]
            - rate * grads.reshape(27, sub, channels)
            + 0.3 * noise[:, rows, :]
        )


def pick(index, arrays):
    return lax.select_n(index, *arrays)


def after(x, *others):
    return lax.optimization_barrier((x, *others))[0]


def quartered_shards(activations, preacts, out_grad, weights, momentum, noise):
    n_dp = lax.axis_size("dp")
    s = lax.axis_index("segment").astype(jnp.int32)
    d = lax.axis_index("dp").astype(jnp.int32)
    ids = jnp.stack([s, d])
    micro, span_t, span_x, span_y, channels = out_grad.shape
    span = (span_t, span_x, span_y)
    rows = micro * span_t * span_x * span_y
    quarter_n = channels // 4
    width = 2 * quarter_n
    half = rows // 2
    per = channels // n_dp
    sub = per // 4
    inputs = activations.reshape(rows, channels)
    pres = preacts.reshape(rows, channels)
    packed = jax.ShapeDtypeStruct((half, width), BF16)
    piece = (3 * sub, 9 * channels)
    columns = pltpu.VMEM((rows, 9 * channels), BF16)

    def array(dtype, *lead):
        return jax.ShapeDtypeStruct(lead + piece, dtype)

    def by_tap(x):
        return jnp.swapaxes(x[0], 0, 1)

    def spread(parts):
        far, one, two = (swapped(parts[m], "segment", m) for m in (3, 1, 2))
        return parts[0], one, two, far

    w_held = spread(
        call(functools.partial(weights_body, per, sub), [array(BF16)] * 4, (ids, by_tap(weights)), 0.9)
    )
    up, *p_parts = call(
        functools.partial(preacts_body, per, sub),
        [packed] * 5,
        (ids, pres, out_grad.reshape(rows, channels)), 1.1,
    )
    p_held = spread(p_parts)

    def far_half(own, *others):
        return jnp.stack([own, after(swapped(own, "dp", 4), *others)])

    def all_chips(pieces, *others):
        return jnp.concatenate([pieces, after(swapped(pieces, "dp", 2), *others)], axis=0)

    def both_cores(pieces):
        other = swapped(pieces, "dp", 1)
        return jnp.concatenate([pieces, other], axis=0).reshape(3 * quarter_n, 9 * channels)

    def terms(field, x):
        return call(
            functools.partial(grads_body, span, n_dp),
            [array(F32, 4), array(BF16, 4)],
            (ids, *field, x), 2.6,
            scratch=[columns, pltpu.VMEM((3 * quarter_n, 9 * channels), F32)],
        )

    def paired(keep, give):
        return call(
            pair_body, [array(F32, 2), array(BF16, 2)], (ids, keep, swapped(give, "dp", 1)), 0.6
        )

    def reduced(stay, send, *others):
        other = after(swapped(send, "dp", 2), *others)
        return call(next_body, [array(F32), array(BF16)], (ids, stay, other), 0.6)

    def summed(own, send):
        return own, swapped(send, "dp", 4)

    def back(section, field, up):
        return call(
            functools.partial(back_body, span, n_dp),
            [packed] * 2,
            (ids, *field, kernels[section], up, pick(s ^ (section - 1), p_held)), 3.0,
            scratch=[columns],
        )

    def tied(field, *others):
        return lax.optimization_barrier((tuple(field), others))[0]

    def tied(field, *others):
        return lax.optimization_barrier((tuple(field), others))[0]

    kernels = {}
    half3 = far_half(after(pick(s ^ 3, w_held), *p_parts))
    chips3 = all_chips(half3)
    kernels[3] = both_cores(chips3)
    field3 = spread(
        call(
            functools.partial(first_body, per, sub),
            [jax.ShapeDtypeStruct((rows, width), BF16)] * 4,
            (ids, up, pick(s ^ 3, p_held), inputs), 6.0,
        )
    )
    x_held = [x[half:] for x in field3]
    half2 = far_half(after(pick(s ^ 2, w_held), half3))
    up, g2 = back(3, field3, up)
    field2 = spread([g2] * 4)
    chips2 = all_chips(half2, g2)
    kernels[2] = both_cores(chips2)
    half1 = far_half(after(pick(s ^ 1, w_held), chips3), g2)
    terms3 = terms(tied(field3, g2), pick(s ^ 3, x_held))
    up, g1 = back(2, tied(field2, terms3), up)
    field1 = spread([g1] * 4)
    chips1 = all_chips(half1, g1)
    kernels[1] = both_cores(chips1)
    terms3 = paired(*tied(terms3, g1))
    terms2 = terms(tied(field2, g1), pick(s ^ 2, x_held))
    up, g0 = back(1, tied(field1, terms2, terms3), up)
    field0 = spread([g0] * 4)
    terms3 = reduced(*terms3, g0)
    terms2 = paired(*tied(terms2, g0))
    terms1 = terms(tied(field1, g0), pick(s ^ 1, x_held))
    terms0 = terms(tied(field0, terms1, terms2, terms3), pick(s, x_held))
    terms1 = paired(*terms1)
    terms0 = paired(*terms0)
    sums = [
        summed(*terms3), summed(*reduced(*terms2)), summed(*reduced(*terms1)), summed(*reduced(*terms0))
    ][::-1]
    owned = spread(
        call(sums_body, [array(BF16)] * 4, (ids, *sums[0], *sums[1], *sums[2], *sums[3]), 0.7)
    )
    rate = 1.0 / math.sqrt(n_dp * rows)
    updated = call(
        functools.partial(update_body, per, sub, rate),
        jax.ShapeDtypeStruct((27, per, channels), F32),
        (ids, *owned, by_tap(momentum), by_tap(noise)), 2.0,
    )
    return jnp.swapaxes(updated, 0, 1)[None]


def solution(mesh):
    placed = (
        P("segment", "dp", None, None, None, None),
        P("segment", "dp", None, None, None, None),
        P("dp", None, None, None, None),
        P("segment", "dp", None, None),
        P("segment", "dp", None, None),
        P("segment", "dp", None, None),
    )

    def shards(activations, preacts, out_grad, weights, momentum, noise):
        channels = weights.shape[-1]
        n_dp = mesh.shape["dp"]
        fits = (
            mesh.shape["segment"] == 4
            and channels % (32 * n_dp) == 0
            and n_dp == 8
            and out_grad.shape[3] == 8
        )
        plan = quartered_shards if fits else general_shards
        return plan(activations, preacts, out_grad, weights, momentum, noise)

    return jax.shard_map(
        shards,
        mesh=mesh,
        in_specs=placed,
        out_specs=P("segment", "dp", None, None),
        check_vma=False,
    )
```

```python
import functools
import math

import jax
import jax.numpy as jnp
from jax import lax
from jax.experimental import pallas as pl
from jax.experimental.pallas import tpu as pltpu
from jax.sharding import PartitionSpec as P

BF16 = jnp.bfloat16
F32 = jnp.float32
VMEM_BYTES = 48 * 1024 * 1024
PEAK_PER_US = 1.1535e9
WEIGHT = 10


def shifted(x, axis, by):
    size = lax.axis_size(axis)
    pairs = [(i, i + by) for i in range(size) if 0 <= i + by < size]
    return lax.ppermute(x, axis, pairs)


def swapped(x, axis, mask):
    return lax.ppermute(x, axis, [(i, i ^ mask) for i in range(lax.axis_size(axis))])


def tap_stack(field, sign):
    batch_n, span_t, span_x, span_y, channels = field.shape
    padded = jnp.pad(field, ((0, 0), (1, 1), (1, 1), (1, 1), (0, 0)))
    views = []
    for along_t in (-1, 0, 1):
        for along_x in (-1, 0, 1):
            for along_y in (-1, 0, 1):
                start_t = 1 + sign * along_t
                start_x = 1 + sign * along_x
                start_y = 1 + sign * along_y
                views.append(
                    padded[
                        :,
                        start_t : start_t + span_t,
                        start_x : start_x + span_x,
                        start_y : start_y + span_y,
                        :,
                    ]
                )
    return jnp.stack(views, axis=4).reshape(batch_n * span_t * span_x * span_y, 27, channels)


def general_shards(activations, preacts, out_grad, weights, momentum, noise):
    segments = lax.axis_size("segment")
    devices_dp = lax.axis_size("dp")
    segment_id = lax.axis_index("segment")
    kernel = lax.all_gather(weights.astype(BF16), "dp", axis=1, tiled=True)[0]
    inputs = activations[0]
    pres = preacts[0]
    micro, span_t, span_x, span_y, channels = inputs.shape
    cells = span_t * span_x * span_y
    is_last = segment_id == segments - 1

    def step_fn(step, carry):
        incoming, total = carry
        index = step - (segments - 1 - segment_id)
        valid = jnp.logical_and(index >= 0, index < micro)
        clipped = jnp.clip(index, 0, micro - 1)
        given = lax.dynamic_index_in_dim(out_grad, clipped, 0, keepdims=False)
        upstream = jnp.where(is_last, given, incoming)
        pre = lax.dynamic_index_in_dim(pres, clipped, 0, keepdims=False).astype(F32)
        sig = jax.nn.sigmoid(pre)
        up_wide = upstream.astype(F32)
        grad_pre = (up_wide * sig * (1.0 + pre * (1.0 - sig)) * valid.astype(F32)).astype(BF16)
        pre_cols = tap_stack(grad_pre[None], -1)
        back = jnp.einsum("nto,cto->nc", pre_cols, kernel, preferred_element_type=F32)
        passed = (up_wide + back.reshape(upstream.shape)).astype(BF16)
        in_cols = tap_stack(lax.dynamic_index_in_dim(inputs, clipped, 0, keepdims=True), 1)
        total = total + jnp.einsum(
            "ntc,no->cto", in_cols, grad_pre.reshape(cells, channels), preferred_element_type=F32
        )
        return shifted(passed, "segment", -1), total

    init = (jnp.zeros(inputs.shape[1:], BF16), jnp.zeros((channels, 27, channels), F32))
    total = lax.fori_loop(0, micro + segments - 1, step_fn, init)[1]
    owned = lax.psum_scatter(total, "dp", scatter_dimension=0, tiled=True)
    rate = 1.0 / math.sqrt(devices_dp * micro * cells)
    return (0.9 * momentum[0] - rate * owned + 0.3 * noise[0])[None]


def iota(shape, dim):
    return lax.broadcasted_iota(jnp.int32, shape, dim)


def log2(n):
    return n.bit_length() - 1


def channel_of(place, quarter, per, sub):
    return (place >> log2(sub)) * per + quarter * sub + (place & (sub - 1))


def dot(a, b):
    return jnp.dot(a, b, preferred_element_type=F32)


def call(body, out_shape, args, us, scratch=()):
    return pl.pallas_call(
        body,
        out_shape=out_shape,
        in_specs=[pl.BlockSpec(memory_space=pltpu.SMEM)]
        + [pl.BlockSpec(memory_space=pltpu.VMEM)] * (len(args) - 1),
        out_specs=jax.tree.map(lambda _: pl.BlockSpec(memory_space=pltpu.VMEM), out_shape),
        scratch_shapes=list(scratch),
        compiler_params=pltpu.CompilerParams(vmem_limit_bytes=VMEM_BYTES),
        cost_estimate=pl.CostEstimate(
            flops=int(us * WEIGHT * PEAK_PER_US), bytes_accessed=0, transcendentals=0
        ),
    )(*args)


def weights_body(per, sub, ids, w_ref, *out_refs):
    channels = w_ref.shape[2]
    quarter_n = channels // 4
    s = ids[0]
    lane = iota((channels, channels), 1)
    place = lane & (quarter_n - 1)
    for m, out_ref in enumerate(out_refs):
        target = s ^ m
        own = w_ref[:, pl.ds(pl.multiple_of(target * sub, sub), sub), :]
        quarter = (lane >> log2(quarter_n)) ^ target
        order = iota((channels, channels), 0) == channel_of(place, quarter, per, sub)
        moved = dot(own.reshape(27 * sub, channels).astype(BF16), order.astype(BF16))
        for bc in range(9):
            part = [moved[(a * 9 + bc) * sub : (a * 9 + bc + 1) * sub] for a in range(3)]
            out_ref[:, bc * channels : (bc + 1) * channels] = jnp.concatenate(part, axis=0).astype(
                BF16
            )


def packing(channels, s, per, sub):
    quarter_n = channels // 4
    shape = (channels, 8 * quarter_n)
    lane = iota(shape, 1)
    place = lane & (quarter_n - 1)
    quarter = (lane >> log2(2 * quarter_n)) ^ s
    hit = iota(shape, 0) == channel_of(place, quarter, per, sub)
    low = (lane & (2 * quarter_n - 1)) < quarter_n
    first = jnp.logical_and(hit, low).astype(BF16)
    second = jnp.logical_and(hit, jnp.logical_not(low)).astype(BF16)
    return first, second


def packed_into(refs, field, first, second):
    half = field.shape[0] // 2
    width = first.shape[1] // 4
    lanes = width * len(refs)
    moved = dot(field[:half], first[:, :lanes]) + dot(field[half:], second[:, :lanes])
    for m, ref in enumerate(refs):
        ref[...] = moved[:, m * width : (m + 1) * width].astype(BF16)


def preacts_body(per, sub, ids, pre_ref, up_ref, up_out, *out_refs):
    first, second = packing(pre_ref.shape[1], ids[0], per, sub)
    packed_into(out_refs, pre_ref, first, second)
    packed_into([up_out], up_ref, first, second)


def first_body(per, sub, ids, up_ref, pre_ref, x_ref, *out_refs):
    half = up_ref.shape[0]
    packed_into([r.at[half:] for r in out_refs], x_ref, *packing(x_ref.shape[1], ids[0], per, sub))
    grad_pre = silu_back(up_ref[...].astype(F32), pre_ref[...])
    for ref in out_refs:
        ref[:half] = grad_pre


def silu_back(up_wide, pre):
    pre = pre.astype(F32)
    sig = jax.nn.sigmoid(pre)
    return (up_wide * sig * (1.0 + pre * (1.0 - sig))).astype(BF16)


def shifts(field, span):
    span_x, span_y = span
    rows, lanes = field.shape
    y = iota((rows, lanes), 0) & (span_y - 1)
    along_y = (
        jnp.where(y == span_y - 1, 0.0, pltpu.roll(field, rows - 1, 0)),
        field,
        jnp.where(y == 0, 0.0, pltpu.roll(field, 1, 0)),
    )
    out = []
    for b in (-1, 0, 1):
        for c in (-1, 0, 1):
            part = along_y[c + 1].reshape(rows // (span_x * span_y), span_x, span_y, lanes)
            edge = jnp.zeros_like(part[:, :1])
            if b == 1:
                part = jnp.concatenate([edge, part[:, :-1]], axis=1)
            elif b == -1:
                part = jnp.concatenate([part[:, 1:], edge], axis=1)
            out.append(part.reshape(rows, lanes))
    return out


def fill_columns(cols, parts, half, span):
    width = parts[0].shape[1]
    quarter_n = width // 2
    channels = 4 * quarter_n
    shape = (4 * width, 2 * channels)
    src, dst = iota(shape, 0), iota(shape, 1)
    m, h, place = src >> log2(width), (src >> log2(quarter_n)) & 1, src & (quarter_n - 1)
    unpack = (dst == h * channels + m * quarter_n + place).astype(BF16)
    both = dot(jnp.concatenate([part[:half] for part in parts], axis=1), unpack)
    field = jnp.concatenate([both[:, :channels], both[:, channels:]], axis=0)
    for k, part in enumerate(shifts(field, span[1:])):
        cols[:, k * channels : (k + 1) * channels] = part.astype(BF16)


def back_body(span, n_dp, ids, g0, g1, g2, g3, w_ref, up_ref, pre_ref, up_out, g_out, cols):
    span_t, span_x, span_y = span
    half, width = up_ref.shape
    quarter_n = width // 2
    sub = quarter_n // n_dp
    rows = 2 * half
    plane = span_x * span_y
    d = ids[1]
    fill_columns(cols, (g0, g1, g2, g3), half, span)
    shape = (3 * quarter_n, 3 * quarter_n)
    dst, src = iota(shape, 0), iota(shape, 1)
    a, place = dst >> log2(quarter_n), dst & (quarter_n - 1)
    apart = (place >> log2(sub)) ^ d
    piece = ((apart >> 2) & 1) + (apart & 2) + (n_dp // 2) * (apart & 1)
    order = src == piece * (3 * sub) + a * sub + (place & (sub - 1))
    kernel = dot(order.astype(BF16), w_ref[...]).astype(BF16)
    terms = lax.dot_general(
        cols[...], kernel, (((1,), (1,)), ((), ())), preferred_element_type=F32
    )
    back = []
    for a in range(3):
        back.append(
            terms[:, a * quarter_n : (a + 1) * quarter_n].reshape(
                rows // (span_t * plane), span_t, plane, quarter_n
            )
        )
    edge = jnp.zeros_like(back[0][:, :1])
    total = (
        back[1]
        + jnp.concatenate([back[0][:, 1:], edge], axis=1)
        + jnp.concatenate([edge, back[2][:, :-1]], axis=1)
    ).reshape(rows, quarter_n)
    total = jnp.concatenate([total[:half], total[half:]], axis=1)
    passed = (up_ref[...].astype(F32) + total).astype(BF16)
    up_out[...] = passed
    g_out[...] = silu_back(passed.astype(F32), pre_ref[...])


def grads_body(span, n_dp, ids, g0, g1, g2, g3, x_ref, keep, give, cols, total):
    span_t, span_x, span_y = span
    half, width = x_ref.shape
    quarter_n = width // 2
    sub = quarter_n // n_dp
    plane = span_x * span_y
    d = ids[1]
    fill_columns(cols, (g0, g1, g2, g3), half, span)
    shape = (width, 2 * width)
    src, dst = iota(shape, 0), iota(shape, 1)
    twice = jnp.logical_and(
        (src & (quarter_n - 1)) == (dst & (quarter_n - 1)),
        (src >> log2(quarter_n)) == (dst >> log2(width)),
    ).astype(BF16)
    both = dot(x_ref[...], twice)
    field = jnp.concatenate([both[:, :width], both[:, width:]], axis=0)
    field = field.reshape(2 * half // (span_t * plane), span_t, plane, width)
    edge = jnp.zeros_like(field[:, :1])
    later = jnp.concatenate([field[:, 1:], edge], axis=1)
    earlier = jnp.concatenate([edge, field[:, :-1]], axis=1)
    left = iota(field.shape, 3) < quarter_n
    taps = jnp.concatenate([jnp.where(left, earlier, field), later], axis=3)
    taps = taps.reshape(2 * half, 2 * width)[:, : 3 * quarter_n].astype(BF16)
    total[...] = lax.dot_general(
        taps, cols[...], (((0,), (0,)), ((), ())), preferred_element_type=F32
    )
    for k in range(n_dp // 2):
        for bit, ref in ((0, keep), (1, give)):
            owner = d ^ (2 * k + bit)
            own = [
                total[pl.ds(pl.multiple_of(a * quarter_n + owner * sub, sub), sub), :]
                for a in range(3)
            ]
            ref[k] = jnp.concatenate(own, axis=0).astype(ref.dtype)


def pair_body(ids, keep, other, stay, send):
    for k in range(keep.shape[0]):
        total = keep[k] + other[k].astype(F32)
        if k % 2 == 0:
            stay[k // 2] = total
        else:
            send[k // 2] = total.astype(BF16)


def next_body(ids, stay, other, own, send):
    own[...] = stay[0] + other[0].astype(F32)
    send[...] = (stay[1] + other[1].astype(F32)).astype(BF16)


def sums_body(ids, *refs):
    ins, outs = refs[:8], refs[8:]
    s = ids[0]
    for section in range(4):
        total = (ins[2 * section][...] + ins[2 * section + 1][...].astype(F32)).astype(BF16)
        for m, out_ref in enumerate(outs):
            @pl.when((s ^ m) == section)
            def _(out_ref=out_ref, total=total):
                out_ref[...] = total


def update_body(per, sub, rate, ids, f0, f1, f2, f3, momentum, noise, out):
    channels = momentum.shape[2]
    quarter_n = channels // 4
    s = ids[0]
    lane = iota((channels, channels), 0)
    for m, f in enumerate((f0, f1, f2, f3)):
        source = s ^ m
        place, quarter = lane & (quarter_n - 1), (lane >> log2(quarter_n)) ^ source
        order = iota((channels, channels), 1) == channel_of(place, quarter, per, sub)
        wide = f[...].astype(F32)
        parts = [
            wide[a * sub : (a + 1) * sub, bc * channels : (bc + 1) * channels]
            for a in range(3)
            for bc in range(9)
        ]
        grads = dot(jnp.concatenate(parts, axis=0).astype(BF16), order.astype(BF16))
        rows = pl.ds(pl.multiple_of(source * sub, sub), sub)
        out[:, rows, :] = (
            0.9 * momentum[:, rows, :]
            - rate * grads.reshape(27, sub, channels)
            + 0.3 * noise[:, rows, :]
        )


def pick(index, arrays):
    return lax.select_n(index, *arrays)


def after(x, *others):
    return lax.optimization_barrier((x, *others))[0]


def quartered_shards(activations, preacts, out_grad, weights, momentum, noise):
    n_dp = lax.axis_size("dp")
    s = lax.axis_index("segment").astype(jnp.int32)
    d = lax.axis_index("dp").astype(jnp.int32)
    ids = jnp.stack([s, d])
    micro, span_t, span_x, span_y, channels = out_grad.shape
    span = (span_t, span_x, span_y)
    rows = micro * span_t * span_x * span_y
    quarter_n = channels // 4
    width = 2 * quarter_n
    half = rows // 2
    per = channels // n_dp
    sub = per // 4
    inputs = activations.reshape(rows, channels)
    pres = preacts.reshape(rows, channels)
    packed = jax.ShapeDtypeStruct((half, width), BF16)
    piece = (3 * sub, 9 * channels)
    columns = pltpu.VMEM((rows, 9 * channels), BF16)

    def array(dtype, *lead):
        return jax.ShapeDtypeStruct(lead + piece, dtype)

    def by_tap(x):
        return jnp.swapaxes(x[0], 0, 1)

    def spread(parts):
        far, one, two = (swapped(parts[m], "segment", m) for m in (3, 1, 2))
        return parts[0], one, two, far

    w_held = spread(
        call(functools.partial(weights_body, per, sub), [array(BF16)] * 4, (ids, by_tap(weights)), 0.9)
    )
    up, *p_parts = call(
        functools.partial(preacts_body, per, sub),
        [packed] * 5,
        (ids, pres, out_grad.reshape(rows, channels)), 1.1,
    )
    p_held = spread(p_parts)

    def far_half(own, *others):
        return jnp.stack([own, after(swapped(own, "dp", 4), *others)])

    def all_chips(pieces, *others):
        return jnp.concatenate([pieces, after(swapped(pieces, "dp", 2), *others)], axis=0)

    def both_cores(pieces):
        other = swapped(pieces, "dp", 1)
        return jnp.concatenate([pieces, other], axis=0).reshape(3 * quarter_n, 9 * channels)

    def terms(field, x):
        return call(
            functools.partial(grads_body, span, n_dp),
            [array(F32, 4), array(BF16, 4)],
            (ids, *field, x), 2.6,
            scratch=[columns, pltpu.VMEM((3 * quarter_n, 9 * channels), F32)],
        )

    def paired(keep, give):
        return call(
            pair_body, [array(F32, 2), array(BF16, 2)], (ids, keep, swapped(give, "dp", 1)), 0.6
        )

    def reduced(stay, send, *others):
        other = after(swapped(send, "dp", 2), *others)
        return call(next_body, [array(F32), array(BF16)], (ids, stay, other), 0.6)

    def summed(own, send):
        return own, swapped(send, "dp", 4)

    def back(section, field, up):
        return call(
            functools.partial(back_body, span, n_dp),
            [packed] * 2,
            (ids, *field, kernels[section], up, pick(s ^ (section - 1), p_held)), 3.0,
            scratch=[columns],
        )

    def tied(field, *others):
        return lax.optimization_barrier((tuple(field), others))[0]

    def tied(field, *others):
        return lax.optimization_barrier((tuple(field), others))[0]

    kernels = {}
    half3 = far_half(after(pick(s ^ 3, w_held), *p_parts))
    chips3 = all_chips(half3)
    kernels[3] = both_cores(chips3)
    field3 = spread(
        call(
            functools.partial(first_body, per, sub),
            [jax.ShapeDtypeStruct((rows, width), BF16)] * 4,
            (ids, up, pick(s ^ 3, p_held), inputs), 6.0,
        )
    )
    x_held = [x[half:] for x in field3]
    half2 = far_half(after(pick(s ^ 2, w_held), half3))
    up, g2 = back(3, field3, up)
    field2 = spread([g2] * 4)
    chips2 = all_chips(half2, g2)
    kernels[2] = both_cores(chips2)
    half1 = far_half(after(pick(s ^ 1, w_held), chips3), g2)
    terms3 = terms(tied(field3, g2), pick(s ^ 3, x_held))
    up, g1 = back(2, tied(field2, terms3), up)
    field1 = spread([g1] * 4)
    chips1 = all_chips(half1, g1)
    kernels[1] = both_cores(chips1)
    terms3 = paired(*tied(terms3, g1))
    terms2 = terms(tied(field2, g1), pick(s ^ 2, x_held))
    up, g0 = back(1, tied(field1, terms2, terms3), up)
    field0 = spread([g0] * 4)
    terms3 = reduced(*terms3, g0)
    terms2 = paired(*tied(terms2, g0))
    terms1 = terms(tied(field1, g0), pick(s ^ 1, x_held))
    terms0 = terms(tied(field0, terms1, terms2, terms3), pick(s, x_held))
    terms1 = paired(*terms1)
    terms0 = paired(*terms0)
    sum3 = summed(*terms3)
    sum2 = summed(*reduced(*terms2, terms0))
    sum1 = summed(*reduced(*terms1, terms0))
    sums = [summed(*reduced(*terms0)), sum1, sum2, sum3]
    owned = spread(
        call(sums_body, [array(BF16)] * 4, (ids, *sums[0], *sums[1], *sums[2], *sums[3]), 0.7)
    )
    rate = 1.0 / math.sqrt(n_dp * rows)
    updated = call(
        functools.partial(update_body, per, sub, rate),
        jax.ShapeDtypeStruct((27, per, channels), F32),
        (ids, *owned, by_tap(momentum), by_tap(noise)), 2.0,
    )
    return jnp.swapaxes(updated, 0, 1)[None]


def solution(mesh):
    placed = (
        P("segment", "dp", None, None, None, None),
        P("segment", "dp", None, None, None, None),
        P("dp", None, None, None, None),
        P("segment", "dp", None, None),
        P("segment", "dp", None, None),
        P("segment", "dp", None, None),
    )

    def shards(activations, preacts, out_grad, weights, momentum, noise):
        channels = weights.shape[-1]
        n_dp = mesh.shape["dp"]
        fits = (
            mesh.shape["segment"] == 4
            and channels % (32 * n_dp) == 0
            and n_dp == 8
            and out_grad.shape[3] == 8
        )
        plan = quartered_shards if fits else general_shards
        return plan(activations, preacts, out_grad, weights, momentum, noise)

    return jax.shard_map(
        shards,
        mesh=mesh,
        in_specs=placed,
        out_specs=P("segment", "dp", None, None),
        check_vma=False,
    )
```

```python
import functools
import math

import jax
import jax.numpy as jnp
from jax import lax
from jax.experimental import pallas as pl
from jax.experimental.pallas import tpu as pltpu
from jax.sharding import PartitionSpec as P

BF16 = jnp.bfloat16
F32 = jnp.float32
VMEM_BYTES = 48 * 1024 * 1024
PEAK_PER_US = 1.1535e9
WEIGHT = 10


def shifted(x, axis, by):
    size = lax.axis_size(axis)
    pairs = [(i, i + by) for i in range(size) if 0 <= i + by < size]
    return lax.ppermute(x, axis, pairs)


def swapped(x, axis, mask):
    return lax.ppermute(x, axis, [(i, i ^ mask) for i in range(lax.axis_size(axis))])


def tap_stack(field, sign):
    batch_n, span_t, span_x, span_y, channels = field.shape
    padded = jnp.pad(field, ((0, 0), (1, 1), (1, 1), (1, 1), (0, 0)))
    views = []
    for along_t in (-1, 0, 1):
        for along_x in (-1, 0, 1):
            for along_y in (-1, 0, 1):
                start_t = 1 + sign * along_t
                start_x = 1 + sign * along_x
                start_y = 1 + sign * along_y
                views.append(
                    padded[
                        :,
                        start_t : start_t + span_t,
                        start_x : start_x + span_x,
                        start_y : start_y + span_y,
                        :,
                    ]
                )
    return jnp.stack(views, axis=4).reshape(batch_n * span_t * span_x * span_y, 27, channels)


def general_shards(activations, preacts, out_grad, weights, momentum, noise):
    segments = lax.axis_size("segment")
    devices_dp = lax.axis_size("dp")
    segment_id = lax.axis_index("segment")
    kernel = lax.all_gather(weights.astype(BF16), "dp", axis=1, tiled=True)[0]
    inputs = activations[0]
    pres = preacts[0]
    micro, span_t, span_x, span_y, channels = inputs.shape
    cells = span_t * span_x * span_y
    is_last = segment_id == segments - 1

    def step_fn(step, carry):
        incoming, total = carry
        index = step - (segments - 1 - segment_id)
        valid = jnp.logical_and(index >= 0, index < micro)
        clipped = jnp.clip(index, 0, micro - 1)
        given = lax.dynamic_index_in_dim(out_grad, clipped, 0, keepdims=False)
        upstream = jnp.where(is_last, given, incoming)
        pre = lax.dynamic_index_in_dim(pres, clipped, 0, keepdims=False).astype(F32)
        sig = jax.nn.sigmoid(pre)
        up_wide = upstream.astype(F32)
        grad_pre = (up_wide * sig * (1.0 + pre * (1.0 - sig)) * valid.astype(F32)).astype(BF16)
        pre_cols = tap_stack(grad_pre[None], -1)
        back = jnp.einsum("nto,cto->nc", pre_cols, kernel, preferred_element_type=F32)
        passed = (up_wide + back.reshape(upstream.shape)).astype(BF16)
        in_cols = tap_stack(lax.dynamic_index_in_dim(inputs, clipped, 0, keepdims=True), 1)
        total = total + jnp.einsum(
            "ntc,no->cto", in_cols, grad_pre.reshape(cells, channels), preferred_element_type=F32
        )
        return shifted(passed, "segment", -1), total

    init = (jnp.zeros(inputs.shape[1:], BF16), jnp.zeros((channels, 27, channels), F32))
    total = lax.fori_loop(0, micro + segments - 1, step_fn, init)[1]
    owned = lax.psum_scatter(total, "dp", scatter_dimension=0, tiled=True)
    rate = 1.0 / math.sqrt(devices_dp * micro * cells)
    return (0.9 * momentum[0] - rate * owned + 0.3 * noise[0])[None]


def iota(shape, dim):
    return lax.broadcasted_iota(jnp.int32, shape, dim)


def log2(n):
    return n.bit_length() - 1


def channel_of(place, quarter, per, sub):
    return (place >> log2(sub)) * per + quarter * sub + (place & (sub - 1))


def dot(a, b):
    return jnp.dot(a, b, preferred_element_type=F32)


def call(body, out_shape, args, us, scratch=()):
    return pl.pallas_call(
        body,
        out_shape=out_shape,
        in_specs=[pl.BlockSpec(memory_space=pltpu.SMEM)]
        + [pl.BlockSpec(memory_space=pltpu.VMEM)] * (len(args) - 1),
        out_specs=jax.tree.map(lambda _: pl.BlockSpec(memory_space=pltpu.VMEM), out_shape),
        scratch_shapes=list(scratch),
        compiler_params=pltpu.CompilerParams(vmem_limit_bytes=VMEM_BYTES),
        cost_estimate=pl.CostEstimate(
            flops=int(us * WEIGHT * PEAK_PER_US), bytes_accessed=0, transcendentals=0
        ),
    )(*args)


def weights_body(per, sub, ids, w_ref, *out_refs):
    channels = w_ref.shape[2]
    quarter_n = channels // 4
    s = ids[0]
    lane = iota((channels, channels), 1)
    place = lane & (quarter_n - 1)
    for m, out_ref in enumerate(out_refs):
        target = s ^ m
        own = w_ref[:, pl.ds(pl.multiple_of(target * sub, sub), sub), :]
        quarter = (lane >> log2(quarter_n)) ^ target
        order = iota((channels, channels), 0) == channel_of(place, quarter, per, sub)
        moved = dot(own.reshape(27 * sub, channels).astype(BF16), order.astype(BF16))
        for bc in range(9):
            part = [moved[(a * 9 + bc) * sub : (a * 9 + bc + 1) * sub] for a in range(3)]
            out_ref[:, bc * channels : (bc + 1) * channels] = jnp.concatenate(part, axis=0).astype(
                BF16
            )


def packing(channels, s, per, sub):
    quarter_n = channels // 4
    shape = (channels, 8 * quarter_n)
    lane = iota(shape, 1)
    place = lane & (quarter_n - 1)
    quarter = (lane >> log2(2 * quarter_n)) ^ s
    hit = iota(shape, 0) == channel_of(place, quarter, per, sub)
    low = (lane & (2 * quarter_n - 1)) < quarter_n
    first = jnp.logical_and(hit, low).astype(BF16)
    second = jnp.logical_and(hit, jnp.logical_not(low)).astype(BF16)
    return first, second


def packed_into(refs, field, first, second):
    half = field.shape[0] // 2
    width = first.shape[1] // 4
    lanes = width * len(refs)
    moved = dot(field[:half], first[:, :lanes]) + dot(field[half:], second[:, :lanes])
    for m, ref in enumerate(refs):
        ref[...] = moved[:, m * width : (m + 1) * width].astype(BF16)


def preacts_body(per, sub, ids, pre_ref, up_ref, up_out, *out_refs):
    first, second = packing(pre_ref.shape[1], ids[0], per, sub)
    packed_into(out_refs, pre_ref, first, second)
    packed_into([up_out], up_ref, first, second)


def first_body(per, sub, ids, up_ref, pre_ref, x_ref, *out_refs):
    half = up_ref.shape[0]
    packed_into([r.at[half:] for r in out_refs], x_ref, *packing(x_ref.shape[1], ids[0], per, sub))
    grad_pre = silu_back(up_ref[...].astype(F32), pre_ref[...])
    for ref in out_refs:
        ref[:half] = grad_pre


def silu_back(up_wide, pre):
    pre = pre.astype(F32)
    sig = jax.nn.sigmoid(pre)
    return (up_wide * sig * (1.0 + pre * (1.0 - sig))).astype(BF16)


def shifts(field, span):
    span_x, span_y = span
    rows, lanes = field.shape
    y = iota((rows, lanes), 0) & (span_y - 1)
    along_y = (
        jnp.where(y == span_y - 1, 0.0, pltpu.roll(field, rows - 1, 0)),
        field,
        jnp.where(y == 0, 0.0, pltpu.roll(field, 1, 0)),
    )
    out = []
    for b in (-1, 0, 1):
        for c in (-1, 0, 1):
            part = along_y[c + 1].reshape(rows // (span_x * span_y), span_x, span_y, lanes)
            edge = jnp.zeros_like(part[:, :1])
            if b == 1:
                part = jnp.concatenate([edge, part[:, :-1]], axis=1)
            elif b == -1:
                part = jnp.concatenate([part[:, 1:], edge], axis=1)
            out.append(part.reshape(rows, lanes))
    return out


def fill_columns(cols, parts, half, span):
    width = parts[0].shape[1]
    quarter_n = width // 2
    channels = 4 * quarter_n
    shape = (4 * width, 2 * channels)
    src, dst = iota(shape, 0), iota(shape, 1)
    m, h, place = src >> log2(width), (src >> log2(quarter_n)) & 1, src & (quarter_n - 1)
    unpack = (dst == h * channels + m * quarter_n + place).astype(BF16)
    both = dot(jnp.concatenate([part[:half] for part in parts], axis=1), unpack)
    field = jnp.concatenate([both[:, :channels], both[:, channels:]], axis=0)
    for k, part in enumerate(shifts(field, span[1:])):
        cols[:, k * channels : (k + 1) * channels] = part.astype(BF16)


def find_back(cols, w_ref, up_ref, pre_ref, up_out, g_out, span, n_dp, d):
    span_t, span_x, span_y = span
    half, width = up_ref.shape
    quarter_n = width // 2
    sub = quarter_n // n_dp
    rows = 2 * half
    plane = span_x * span_y
    shape = (3 * quarter_n, 3 * quarter_n)
    dst, src = iota(shape, 0), iota(shape, 1)
    a, place = dst >> log2(quarter_n), dst & (quarter_n - 1)
    apart = (place >> log2(sub)) ^ d
    piece = ((apart >> 2) & 1) + (apart & 2) + (n_dp // 2) * (apart & 1)
    order = src == piece * (3 * sub) + a * sub + (place & (sub - 1))
    kernel = dot(order.astype(BF16), w_ref[...]).astype(BF16)
    terms = lax.dot_general(
        cols[...], kernel, (((1,), (1,)), ((), ())), preferred_element_type=F32
    )
    back = []
    for a in range(3):
        back.append(
            terms[:, a * quarter_n : (a + 1) * quarter_n].reshape(
                rows // (span_t * plane), span_t, plane, quarter_n
            )
        )
    edge = jnp.zeros_like(back[0][:, :1])
    total = (
        back[1]
        + jnp.concatenate([back[0][:, 1:], edge], axis=1)
        + jnp.concatenate([edge, back[2][:, :-1]], axis=1)
    ).reshape(rows, quarter_n)
    total = jnp.concatenate([total[:half], total[half:]], axis=1)
    passed = (up_ref[...].astype(F32) + total).astype(BF16)
    up_out[...] = passed
    g_out[...] = silu_back(passed.astype(F32), pre_ref[...])


def find_terms(cols, x_ref, keep, give, total, span, n_dp, d):
    span_t, span_x, span_y = span
    half, width = x_ref.shape
    quarter_n = width // 2
    sub = quarter_n // n_dp
    plane = span_x * span_y
    shape = (width, 2 * width)
    src, dst = iota(shape, 0), iota(shape, 1)
    twice = jnp.logical_and(
        (src & (quarter_n - 1)) == (dst & (quarter_n - 1)),
        (src >> log2(quarter_n)) == (dst >> log2(width)),
    ).astype(BF16)
    both = dot(x_ref[...], twice)
    field = jnp.concatenate([both[:, :width], both[:, width:]], axis=0)
    field = field.reshape(2 * half // (span_t * plane), span_t, plane, width)
    edge = jnp.zeros_like(field[:, :1])
    later = jnp.concatenate([field[:, 1:], edge], axis=1)
    earlier = jnp.concatenate([edge, field[:, :-1]], axis=1)
    left = iota(field.shape, 3) < quarter_n
    taps = jnp.concatenate([jnp.where(left, earlier, field), later], axis=3)
    taps = taps.reshape(2 * half, 2 * width)[:, : 3 * quarter_n].astype(BF16)
    total[...] = lax.dot_general(
        taps, cols[...], (((0,), (0,)), ((), ())), preferred_element_type=F32
    )
    for k in range(n_dp // 2):
        for bit, ref in ((0, keep), (1, give)):
            owner = d ^ (2 * k + bit)
            own = [
                total[pl.ds(pl.multiple_of(a * quarter_n + owner * sub, sub), sub), :]
                for a in range(3)
            ]
            ref[k] = jnp.concatenate(own, axis=0).astype(ref.dtype)


def back_body(span, n_dp, ids, g0, g1, g2, g3, w_ref, up_ref, pre_ref, up_out, g_out, cols):
    fill_columns(cols, (g0, g1, g2, g3), up_ref.shape[0], span)
    find_back(cols, w_ref, up_ref, pre_ref, up_out, g_out, span, n_dp, ids[1])


def section_body(
    span, n_dp, ids, g0, g1, g2, g3, w_ref, up_ref, pre_ref, x_ref, up_out, g_out, keep, give, cols, total
):
    fill_columns(cols, (g0, g1, g2, g3), up_ref.shape[0], span)
    find_back(cols, w_ref, up_ref, pre_ref, up_out, g_out, span, n_dp, ids[1])
    find_terms(cols, x_ref, keep, give, total, span, n_dp, ids[1])


def terms_body(span, n_dp, ids, g0, g1, g2, g3, x_ref, keep, give, cols, total):
    fill_columns(cols, (g0, g1, g2, g3), x_ref.shape[0], span)
    find_terms(cols, x_ref, keep, give, total, span, n_dp, ids[1])


def pair_body(ids, keep, other, stay, send):
    for k in range(keep.shape[0]):
        total = keep[k] + other[k].astype(F32)
        if k % 2 == 0:
            stay[k // 2] = total
        else:
            send[k // 2] = total.astype(BF16)


def next_body(ids, stay, other, own, send):
    own[...] = stay[0] + other[0].astype(F32)
    send[...] = (stay[1] + other[1].astype(F32)).astype(BF16)


def sums_body(ids, *refs):
    ins, outs = refs[:8], refs[8:]
    s = ids[0]
    for section in range(4):
        total = (ins[2 * section][...] + ins[2 * section + 1][...].astype(F32)).astype(BF16)
        for m, out_ref in enumerate(outs):
            @pl.when((s ^ m) == section)
            def _(out_ref=out_ref, total=total):
                out_ref[...] = total


def update_body(per, sub, rate, ids, f0, f1, f2, f3, momentum, noise, out):
    channels = momentum.shape[2]
    quarter_n = channels // 4
    s = ids[0]
    lane = iota((channels, channels), 0)
    for m, f in enumerate((f0, f1, f2, f3)):
        source = s ^ m
        place, quarter = lane & (quarter_n - 1), (lane >> log2(quarter_n)) ^ source
        order = iota((channels, channels), 1) == channel_of(place, quarter, per, sub)
        wide = f[...].astype(F32)
        parts = [
            wide[a * sub : (a + 1) * sub, bc * channels : (bc + 1) * channels]
            for a in range(3)
            for bc in range(9)
        ]
        grads = dot(jnp.concatenate(parts, axis=0).astype(BF16), order.astype(BF16))
        rows = pl.ds(pl.multiple_of(source * sub, sub), sub)
        out[:, rows, :] = (
            0.9 * momentum[:, rows, :]
            - rate * grads.reshape(27, sub, channels)
            + 0.3 * noise[:, rows, :]
        )


def pick(index, arrays):
    return lax.select_n(index, *arrays)


def after(x, *others):
    return lax.optimization_barrier((x, *others))[0]


def quartered_shards(activations, preacts, out_grad, weights, momentum, noise):
    n_dp = lax.axis_size("dp")
    s = lax.axis_index("segment").astype(jnp.int32)
    d = lax.axis_index("dp").astype(jnp.int32)
    ids = jnp.stack([s, d])
    micro, span_t, span_x, span_y, channels = out_grad.shape
    span = (span_t, span_x, span_y)
    rows = micro * span_t * span_x * span_y
    quarter_n = channels // 4
    width = 2 * quarter_n
    half = rows // 2
    per = channels // n_dp
    sub = per // 4
    inputs = activations.reshape(rows, channels)
    pres = preacts.reshape(rows, channels)
    packed = jax.ShapeDtypeStruct((half, width), BF16)
    piece = (3 * sub, 9 * channels)
    columns = pltpu.VMEM((rows, 9 * channels), BF16)

    def array(dtype, *lead):
        return jax.ShapeDtypeStruct(lead + piece, dtype)

    def by_tap(x):
        return jnp.swapaxes(x[0], 0, 1)

    def spread(parts):
        far, one, two = (swapped(parts[m], "segment", m) for m in (3, 1, 2))
        return parts[0], one, two, far

    w_held = spread(
        call(functools.partial(weights_body, per, sub), [array(BF16)] * 4, (ids, by_tap(weights)), 0.9)
    )
    up, *p_parts = call(
        functools.partial(preacts_body, per, sub),
        [packed] * 5,
        (ids, pres, out_grad.reshape(rows, channels)), 1.1,
    )
    p_held = spread(p_parts)

    def far_half(own, *others):
        return jnp.stack([own, after(swapped(own, "dp", 4), *others)])

    def all_chips(pieces, *others):
        return jnp.concatenate([pieces, after(swapped(pieces, "dp", 2), *others)], axis=0)

    def both_cores(pieces):
        other = swapped(pieces, "dp", 1)
        return jnp.concatenate([pieces, other], axis=0).reshape(3 * quarter_n, 9 * channels)

    def terms(field, x):
        return call(
            functools.partial(terms_body, span, n_dp),
            [array(F32, 4), array(BF16, 4)],
            (ids, *field, x), 2.6,
            scratch=[columns, pltpu.VMEM((3 * quarter_n, 9 * channels), F32)],
        )

    def paired(keep, give):
        return call(
            pair_body, [array(F32, 2), array(BF16, 2)], (ids, keep, swapped(give, "dp", 1)), 0.6
        )

    def reduced(stay, send, *others):
        other = after(swapped(send, "dp", 2), *others)
        return call(next_body, [array(F32), array(BF16)], (ids, stay, other), 0.6)

    def summed(own, send):
        return own, swapped(send, "dp", 4)

    def back(section, field, up):
        return call(
            functools.partial(back_body, span, n_dp),
            [packed] * 2,
            (ids, *field, kernels[section], up, pick(s ^ (section - 1), p_held)), 3.0,
            scratch=[columns],
        )

    def back_and_terms(section, field, up):
        up, g, *terms = call(
            functools.partial(section_body, span, n_dp),
            [packed, packed, array(F32, 4), array(BF16, 4)],
            (
                ids, *field, kernels[section], up,
                pick(s ^ (section - 1), p_held), pick(s ^ section, x_held),
            ), 3.8,
            scratch=[columns, pltpu.VMEM((3 * quarter_n, 9 * channels), F32)],
        )
        return up, g, terms

    def tied(field, *others):
        return lax.optimization_barrier((tuple(field), others))[0]

    def tied(field, *others):
        return lax.optimization_barrier((tuple(field), others))[0]

    kernels = {}
    first = call(
        functools.partial(first_body, per, sub),
        [jax.ShapeDtypeStruct((rows, width), BF16)] * 4,
        (ids, up, pick(s ^ 3, p_held), inputs), 1.1,
    )
    field3 = spread(first)
    half3 = far_half(after(pick(s ^ 3, w_held), *p_parts))
    chips3 = all_chips(after(half3, first[0]))
    kernels[3] = both_cores(chips3)
    x_held = [x[half:] for x in field3]
    half2 = far_half(after(pick(s ^ 2, w_held), half3, first[0]))
    up, g2 = back(3, field3, up)
    field2 = spread([g2] * 4)
    chips2 = all_chips(half2, g2)
    kernels[2] = both_cores(chips2)
    half1 = far_half(after(pick(s ^ 1, w_held), chips3), g2)
    terms3 = terms(tied(field3, g2), pick(s ^ 3, x_held))
    up, g1 = back(2, tied(field2, terms3), up)
    field1 = spread([g1] * 4)
    chips1 = all_chips(half1, g1)
    kernels[1] = both_cores(chips1)
    terms3 = paired(*tied(terms3, g1))
    terms2 = terms(tied(field2, g1), pick(s ^ 2, x_held))
    terms2 = paired(*terms2)
    up, g0, terms1 = back_and_terms(1, tied(field1, terms2, terms3), up)
    field0 = spread([g0] * 4)
    terms3 = reduced(*terms3, g0)
    terms1 = paired(*terms1)
    terms0 = terms(tied(field0, terms1, terms3), pick(s, x_held))
    terms0 = paired(*terms0)
    sum3 = summed(*terms3)
    terms2 = reduced(*terms2)
    terms1 = reduced(*terms1)
    terms0 = reduced(*terms0)
    sums = [summed(*terms0), summed(*terms1), summed(*terms2), sum3]
    owned = spread(
        call(sums_body, [array(BF16)] * 4, (ids, *sums[0], *sums[1], *sums[2], *sums[3]), 0.7)
    )
    rate = 1.0 / math.sqrt(n_dp * rows)
    updated = call(
        functools.partial(update_body, per, sub, rate),
        jax.ShapeDtypeStruct((27, per, channels), F32),
        (ids, *owned, by_tap(momentum), by_tap(noise)), 2.0,
    )
    return jnp.swapaxes(updated, 0, 1)[None]


def solution(mesh):
    placed = (
        P("segment", "dp", None, None, None, None),
        P("segment", "dp", None, None, None, None),
        P("dp", None, None, None, None),
        P("segment", "dp", None, None),
        P("segment", "dp", None, None),
        P("segment", "dp", None, None),
    )

    def shards(activations, preacts, out_grad, weights, momentum, noise):
        channels = weights.shape[-1]
        n_dp = mesh.shape["dp"]
        fits = (
            mesh.shape["segment"] == 4
            and channels % (32 * n_dp) == 0
            and n_dp == 8
            and out_grad.shape[3] == 8
        )
        plan = quartered_shards if fits else general_shards
        return plan(activations, preacts, out_grad, weights, momentum, noise)

    return jax.shard_map(
        shards,
        mesh=mesh,
        in_specs=placed,
        out_specs=P("segment", "dp", None, None),
        check_vma=False,
    )
```

```python
import functools
import math

import jax
import jax.numpy as jnp
from jax import lax
from jax.experimental import pallas as pl
from jax.experimental.pallas import tpu as pltpu
from jax.sharding import PartitionSpec as P

BF16 = jnp.bfloat16
F32 = jnp.float32
VMEM_BYTES = 48 * 1024 * 1024
PEAK_PER_US = 1.1535e9
WEIGHT = 10


def shifted(x, axis, by):
    size = lax.axis_size(axis)
    pairs = [(i, i + by) for i in range(size) if 0 <= i + by < size]
    return lax.ppermute(x, axis, pairs)


def swapped(x, axis, mask):
    return lax.ppermute(x, axis, [(i, i ^ mask) for i in range(lax.axis_size(axis))])


def tap_stack(field, sign):
    batch_n, span_t, span_x, span_y, channels = field.shape
    padded = jnp.pad(field, ((0, 0), (1, 1), (1, 1), (1, 1), (0, 0)))
    views = []
    for along_t in (-1, 0, 1):
        for along_x in (-1, 0, 1):
            for along_y in (-1, 0, 1):
                start_t = 1 + sign * along_t
                start_x = 1 + sign * along_x
                start_y = 1 + sign * along_y
                views.append(
                    padded[
                        :,
                        start_t : start_t + span_t,
                        start_x : start_x + span_x,
                        start_y : start_y + span_y,
                        :,
                    ]
                )
    return jnp.stack(views, axis=4).reshape(batch_n * span_t * span_x * span_y, 27, channels)


def general_shards(activations, preacts, out_grad, weights, momentum, noise):
    segments = lax.axis_size("segment")
    devices_dp = lax.axis_size("dp")
    segment_id = lax.axis_index("segment")
    kernel = lax.all_gather(weights.astype(BF16), "dp", axis=1, tiled=True)[0]
    inputs = activations[0]
    pres = preacts[0]
    micro, span_t, span_x, span_y, channels = inputs.shape
    cells = span_t * span_x * span_y
    is_last = segment_id == segments - 1

    def step_fn(step, carry):
        incoming, total = carry
        index = step - (segments - 1 - segment_id)
        valid = jnp.logical_and(index >= 0, index < micro)
        clipped = jnp.clip(index, 0, micro - 1)
        given = lax.dynamic_index_in_dim(out_grad, clipped, 0, keepdims=False)
        upstream = jnp.where(is_last, given, incoming)
        pre = lax.dynamic_index_in_dim(pres, clipped, 0, keepdims=False).astype(F32)
        sig = jax.nn.sigmoid(pre)
        up_wide = upstream.astype(F32)
        grad_pre = (up_wide * sig * (1.0 + pre * (1.0 - sig)) * valid.astype(F32)).astype(BF16)
        pre_cols = tap_stack(grad_pre[None], -1)
        back = jnp.einsum("nto,cto->nc", pre_cols, kernel, preferred_element_type=F32)
        passed = (up_wide + back.reshape(upstream.shape)).astype(BF16)
        in_cols = tap_stack(lax.dynamic_index_in_dim(inputs, clipped, 0, keepdims=True), 1)
        total = total + jnp.einsum(
            "ntc,no->cto", in_cols, grad_pre.reshape(cells, channels), preferred_element_type=F32
        )
        return shifted(passed, "segment", -1), total

    init = (jnp.zeros(inputs.shape[1:], BF16), jnp.zeros((channels, 27, channels), F32))
    total = lax.fori_loop(0, micro + segments - 1, step_fn, init)[1]
    owned = lax.psum_scatter(total, "dp", scatter_dimension=0, tiled=True)
    rate = 1.0 / math.sqrt(devices_dp * micro * cells)
    return (0.9 * momentum[0] - rate * owned + 0.3 * noise[0])[None]


def iota(shape, dim):
    return lax.broadcasted_iota(jnp.int32, shape, dim)


def log2(n):
    return n.bit_length() - 1


def channel_of(place, quarter, per, sub):
    return (place >> log2(sub)) * per + quarter * sub + (place & (sub - 1))


def dot(a, b):
    return jnp.dot(a, b, preferred_element_type=F32)


def call(body, out_shape, args, us, scratch=()):
    return pl.pallas_call(
        body,
        out_shape=out_shape,
        in_specs=[pl.BlockSpec(memory_space=pltpu.SMEM)]
        + [pl.BlockSpec(memory_space=pltpu.VMEM)] * (len(args) - 1),
        out_specs=jax.tree.map(lambda _: pl.BlockSpec(memory_space=pltpu.VMEM), out_shape),
        scratch_shapes=list(scratch),
        compiler_params=pltpu.CompilerParams(vmem_limit_bytes=VMEM_BYTES),
        cost_estimate=pl.CostEstimate(
            flops=int(us * WEIGHT * PEAK_PER_US), bytes_accessed=0, transcendentals=0
        ),
    )(*args)


def weights_body(per, sub, ids, w_ref, *out_refs):
    channels = w_ref.shape[2]
    quarter_n = channels // 4
    s = ids[0]
    lane = iota((channels, channels), 1)
    place = lane & (quarter_n - 1)
    for m, out_ref in enumerate(out_refs):
        target = s ^ m
        own = w_ref[:, pl.ds(pl.multiple_of(target * sub, sub), sub), :]
        quarter = (lane >> log2(quarter_n)) ^ target
        order = iota((channels, channels), 0) == channel_of(place, quarter, per, sub)
        moved = dot(own.reshape(27 * sub, channels).astype(BF16), order.astype(BF16))
        for bc in range(9):
            part = [moved[(a * 9 + bc) * sub : (a * 9 + bc + 1) * sub] for a in range(3)]
            out_ref[:, bc * channels : (bc + 1) * channels] = jnp.concatenate(part, axis=0).astype(
                BF16
            )


def packing(channels, s, per, sub):
    quarter_n = channels // 4
    shape = (channels, 8 * quarter_n)
    lane = iota(shape, 1)
    place = lane & (quarter_n - 1)
    quarter = (lane >> log2(2 * quarter_n)) ^ s
    hit = iota(shape, 0) == channel_of(place, quarter, per, sub)
    low = (lane & (2 * quarter_n - 1)) < quarter_n
    first = jnp.logical_and(hit, low).astype(BF16)
    second = jnp.logical_and(hit, jnp.logical_not(low)).astype(BF16)
    return first, second


def packed_into(refs, field, first, second):
    half = field.shape[0] // 2
    width = first.shape[1] // 4
    lanes = width * len(refs)
    moved = dot(field[:half], first[:, :lanes]) + dot(field[half:], second[:, :lanes])
    for m, ref in enumerate(refs):
        ref[...] = moved[:, m * width : (m + 1) * width].astype(BF16)


def preacts_body(per, sub, ids, pre_ref, up_ref, up_out, *out_refs):
    first, second = packing(pre_ref.shape[1], ids[0], per, sub)
    packed_into(out_refs, pre_ref, first, second)
    packed_into([up_out], up_ref, first, second)


def first_body(per, sub, ids, up_ref, pre_ref, x_ref, *out_refs):
    half = up_ref.shape[0]
    packed_into([r.at[half:] for r in out_refs], x_ref, *packing(x_ref.shape[1], ids[0], per, sub))
    grad_pre = silu_back(up_ref[...].astype(F32), pre_ref[...])
    for ref in out_refs:
        ref[:half] = grad_pre


def silu_back(up_wide, pre):
    pre = pre.astype(F32)
    sig = jax.nn.sigmoid(pre)
    return (up_wide * sig * (1.0 + pre * (1.0 - sig))).astype(BF16)


def shifts(field, span):
    span_x, span_y = span
    rows, lanes = field.shape
    y = iota((rows, lanes), 0) & (span_y - 1)
    along_y = (
        jnp.where(y == span_y - 1, 0.0, pltpu.roll(field, rows - 1, 0)),
        field,
        jnp.where(y == 0, 0.0, pltpu.roll(field, 1, 0)),
    )
    out = []
    for b in (-1, 0, 1):
        for c in (-1, 0, 1):
            part = along_y[c + 1].reshape(rows // (span_x * span_y), span_x, span_y, lanes)
            edge = jnp.zeros_like(part[:, :1])
            if b == 1:
                part = jnp.concatenate([edge, part[:, :-1]], axis=1)
            elif b == -1:
                part = jnp.concatenate([part[:, 1:], edge], axis=1)
            out.append(part.reshape(rows, lanes))
    return out


def fill_columns(cols, parts, half, span):
    width = parts[0].shape[1]
    quarter_n = width // 2
    channels = 4 * quarter_n
    shape = (4 * width, 2 * channels)
    src, dst = iota(shape, 0), iota(shape, 1)
    m, h, place = src >> log2(width), (src >> log2(quarter_n)) & 1, src & (quarter_n - 1)
    unpack = (dst == h * channels + m * quarter_n + place).astype(BF16)
    both = dot(jnp.concatenate([part[:half] for part in parts], axis=1), unpack)
    field = jnp.concatenate([both[:, :channels], both[:, channels:]], axis=0)
    for k, part in enumerate(shifts(field, span[1:])):
        cols[:, k * channels : (k + 1) * channels] = part.astype(BF16)


def find_back(cols, w_ref, up_ref, pre_ref, up_out, g_out, span, n_dp, d):
    span_t, span_x, span_y = span
    half, width = up_ref.shape
    quarter_n = width // 2
    sub = quarter_n // n_dp
    rows = 2 * half
    plane = span_x * span_y
    shape = (3 * quarter_n, 3 * quarter_n)
    dst, src = iota(shape, 0), iota(shape, 1)
    a, place = dst >> log2(quarter_n), dst & (quarter_n - 1)
    apart = (place >> log2(sub)) ^ d
    piece = ((apart >> 2) & 1) + (apart & 2) + (n_dp // 2) * (apart & 1)
    order = src == piece * (3 * sub) + a * sub + (place & (sub - 1))
    kernel = dot(order.astype(BF16), w_ref[...]).astype(BF16)
    terms = lax.dot_general(
        cols[...], kernel, (((1,), (1,)), ((), ())), preferred_element_type=F32
    )
    back = []
    for a in range(3):
        back.append(
            terms[:, a * quarter_n : (a + 1) * quarter_n].reshape(
                rows // (span_t * plane), span_t, plane, quarter_n
            )
        )
    edge = jnp.zeros_like(back[0][:, :1])
    total = (
        back[1]
        + jnp.concatenate([back[0][:, 1:], edge], axis=1)
        + jnp.concatenate([edge, back[2][:, :-1]], axis=1)
    ).reshape(rows, quarter_n)
    total = jnp.concatenate([total[:half], total[half:]], axis=1)
    passed = (up_ref[...].astype(F32) + total).astype(BF16)
    up_out[...] = passed
    g_out[...] = silu_back(passed.astype(F32), pre_ref[...])


def find_terms(cols, x_ref, keep, give, total, span, n_dp, d):
    span_t, span_x, span_y = span
    half, width = x_ref.shape
    quarter_n = width // 2
    sub = quarter_n // n_dp
    plane = span_x * span_y
    shape = (width, 2 * width)
    src, dst = iota(shape, 0), iota(shape, 1)
    twice = jnp.logical_and(
        (src & (quarter_n - 1)) == (dst & (quarter_n - 1)),
        (src >> log2(quarter_n)) == (dst >> log2(width)),
    ).astype(BF16)
    both = dot(x_ref[...], twice)
    field = jnp.concatenate([both[:, :width], both[:, width:]], axis=0)
    field = field.reshape(2 * half // (span_t * plane), span_t, plane, width)
    edge = jnp.zeros_like(field[:, :1])
    later = jnp.concatenate([field[:, 1:], edge], axis=1)
    earlier = jnp.concatenate([edge, field[:, :-1]], axis=1)
    left = iota(field.shape, 3) < quarter_n
    taps = jnp.concatenate([jnp.where(left, earlier, field), later], axis=3)
    taps = taps.reshape(2 * half, 2 * width)[:, : 3 * quarter_n].astype(BF16)
    total[...] = lax.dot_general(
        taps, cols[...], (((0,), (0,)), ((), ())), preferred_element_type=F32
    )
    for k in range(n_dp // 2):
        for bit, ref in ((0, keep), (1, give)):
            owner = d ^ (2 * k + bit)
            own = [
                total[pl.ds(pl.multiple_of(a * quarter_n + owner * sub, sub), sub), :]
                for a in range(3)
            ]
            ref[k] = jnp.concatenate(own, axis=0).astype(ref.dtype)


def back_body(span, n_dp, ids, g0, g1, g2, g3, w_ref, up_ref, pre_ref, up_out, g_out, cols):
    fill_columns(cols, (g0, g1, g2, g3), up_ref.shape[0], span)
    find_back(cols, w_ref, up_ref, pre_ref, up_out, g_out, span, n_dp, ids[1])


def section_body(
    span, n_dp, ids, g0, g1, g2, g3, w_ref, up_ref, pre_ref, x_ref, up_out, g_out, keep, give, cols, total
):
    fill_columns(cols, (g0, g1, g2, g3), up_ref.shape[0], span)
    find_back(cols, w_ref, up_ref, pre_ref, up_out, g_out, span, n_dp, ids[1])
    find_terms(cols, x_ref, keep, give, total, span, n_dp, ids[1])


def terms_body(span, n_dp, ids, g0, g1, g2, g3, x_ref, keep, give, cols, total):
    fill_columns(cols, (g0, g1, g2, g3), x_ref.shape[0], span)
    find_terms(cols, x_ref, keep, give, total, span, n_dp, ids[1])


def pair_body(ids, keep, other, stay, send):
    for k in range(keep.shape[0]):
        total = keep[k] + other[k].astype(F32)
        if k % 2 == 0:
            stay[k // 2] = total
        else:
            send[k // 2] = total.astype(BF16)


def next_body(ids, stay, other, own, send):
    own[...] = stay[0] + other[0].astype(F32)
    send[...] = (stay[1] + other[1].astype(F32)).astype(BF16)


def sums_body(ids, *refs):
    ins, outs = refs[:8], refs[8:]
    s = ids[0]
    for section in range(4):
        total = (ins[2 * section][...] + ins[2 * section + 1][...].astype(F32)).astype(BF16)
        for m, out_ref in enumerate(outs):
            @pl.when((s ^ m) == section)
            def _(out_ref=out_ref, total=total):
                out_ref[...] = total


def update_body(per, sub, rate, ids, f0, f1, f2, f3, momentum, noise, out):
    channels = momentum.shape[2]
    quarter_n = channels // 4
    s = ids[0]
    lane = iota((channels, channels), 0)
    for m, f in enumerate((f0, f1, f2, f3)):
        source = s ^ m
        place, quarter = lane & (quarter_n - 1), (lane >> log2(quarter_n)) ^ source
        order = iota((channels, channels), 1) == channel_of(place, quarter, per, sub)
        wide = f[...].astype(F32)
        parts = [
            wide[a * sub : (a + 1) * sub, bc * channels : (bc + 1) * channels]
            for a in range(3)
            for bc in range(9)
        ]
        grads = dot(jnp.concatenate(parts, axis=0).astype(BF16), order.astype(BF16))
        rows = pl.ds(pl.multiple_of(source * sub, sub), sub)
        out[:, rows, :] = (
            0.9 * momentum[:, rows, :]
            - rate * grads.reshape(27, sub, channels)
            + 0.3 * noise[:, rows, :]
        )


def pick(index, arrays):
    return lax.select_n(index, *arrays)


def after(x, *others):
    return lax.optimization_barrier((x, *others))[0]


def quartered_shards(activations, preacts, out_grad, weights, momentum, noise):
    n_dp = lax.axis_size("dp")
    s = lax.axis_index("segment").astype(jnp.int32)
    d = lax.axis_index("dp").astype(jnp.int32)
    ids = jnp.stack([s, d])
    micro, span_t, span_x, span_y, channels = out_grad.shape
    span = (span_t, span_x, span_y)
    rows = micro * span_t * span_x * span_y
    quarter_n = channels // 4
    width = 2 * quarter_n
    half = rows // 2
    per = channels // n_dp
    sub = per // 4
    inputs = activations.reshape(rows, channels)
    pres = preacts.reshape(rows, channels)
    packed = jax.ShapeDtypeStruct((half, width), BF16)
    piece = (3 * sub, 9 * channels)
    columns = pltpu.VMEM((rows, 9 * channels), BF16)

    def array(dtype, *lead):
        return jax.ShapeDtypeStruct(lead + piece, dtype)

    def by_tap(x):
        return jnp.swapaxes(x[0], 0, 1)

    def spread(parts):
        far, one, two = (swapped(parts[m], "segment", m) for m in (3, 1, 2))
        return parts[0], one, two, far

    w_held = spread(
        call(functools.partial(weights_body, per, sub), [array(BF16)] * 4, (ids, by_tap(weights)), 0.9)
    )
    up, *p_parts = call(
        functools.partial(preacts_body, per, sub),
        [packed] * 5,
        (ids, pres, out_grad.reshape(rows, channels)), 1.1,
    )
    p_held = spread(p_parts)

    def far_half(own, *others):
        return jnp.stack([own, after(swapped(own, "dp", 4), *others)])

    def all_chips(pieces, *others):
        return jnp.concatenate([pieces, after(swapped(pieces, "dp", 2), *others)], axis=0)

    def both_cores(pieces):
        other = swapped(pieces, "dp", 1)
        return jnp.concatenate([pieces, other], axis=0).reshape(3 * quarter_n, 9 * channels)

    def terms(field, x):
        return call(
            functools.partial(terms_body, span, n_dp),
            [array(F32, 4), array(BF16, 4)],
            (ids, *field, x), 2.6,
            scratch=[columns, pltpu.VMEM((3 * quarter_n, 9 * channels), F32)],
        )

    def paired(keep, give):
        return call(
            pair_body, [array(F32, 2), array(BF16, 2)], (ids, keep, swapped(give, "dp", 1)), 0.6
        )

    def reduced(stay, send, *others):
        other = after(swapped(send, "dp", 2), *others)
        return call(next_body, [array(F32), array(BF16)], (ids, stay, other), 0.6)

    def summed(own, send):
        return own, swapped(send, "dp", 4)

    def back(section, field, up):
        return call(
            functools.partial(back_body, span, n_dp),
            [packed] * 2,
            (ids, *field, kernels[section], up, pick(s ^ (section - 1), p_held)), 3.0,
            scratch=[columns],
        )

    def back_and_terms(section, field, up):
        up, g, *terms = call(
            functools.partial(section_body, span, n_dp),
            [packed, packed, array(F32, 4), array(BF16, 4)],
            (
                ids, *field, kernels[section], up,
                pick(s ^ (section - 1), p_held), pick(s ^ section, x_held),
            ), 3.8,
            scratch=[columns, pltpu.VMEM((3 * quarter_n, 9 * channels), F32)],
        )
        return up, g, terms

    def tied(field, *others):
        return lax.optimization_barrier((tuple(field), others))[0]

    def tied(field, *others):
        return lax.optimization_barrier((tuple(field), others))[0]

    kernels = {}
    first = call(
        functools.partial(first_body, per, sub),
        [jax.ShapeDtypeStruct((rows, width), BF16)] * 4,
        (ids, up, pick(s ^ 3, p_held), inputs), 1.1,
    )
    field3 = spread(first)
    half3 = far_half(after(pick(s ^ 3, w_held), *p_parts))
    chips3 = all_chips(after(half3, first[0]))
    kernels[3] = both_cores(chips3)
    x_held = [x[half:] for x in field3]
    half2 = far_half(after(pick(s ^ 2, w_held), half3, first[0]))
    up, g2 = back(3, field3, up)
    field2 = spread([g2] * 4)
    chips2 = all_chips(half2, g2)
    kernels[2] = both_cores(chips2)
    half1 = far_half(after(pick(s ^ 1, w_held), chips3), g2)
    terms3 = terms(tied(field3, g2), pick(s ^ 3, x_held))
    up, g1 = back(2, tied(field2, terms3), up)
    field1 = spread([g1] * 4)
    chips1 = all_chips(half1, g1)
    kernels[1] = both_cores(chips1)
    terms3 = paired(*tied(terms3, g1))
    terms2 = terms(tied(field2, g1), pick(s ^ 2, x_held))
    terms2 = paired(*terms2)
    up, g0, terms1 = back_and_terms(1, tied(field1, terms2, terms3), up)
    field0 = spread([g0] * 4)
    terms1 = paired(*terms1)
    terms0 = terms(tied(field0, terms1), pick(s, x_held))
    terms3 = reduced(*terms3, terms0[0])
    terms0 = paired(*terms0)
    sum3 = summed(*terms3)
    terms2 = reduced(*terms2)
    terms1 = reduced(*terms1, terms0)
    terms0 = reduced(*terms0)
    sums = [summed(*terms0), summed(*terms1), summed(*terms2), sum3]
    owned = spread(
        call(sums_body, [array(BF16)] * 4, (ids, *sums[0], *sums[1], *sums[2], *sums[3]), 0.7)
    )
    rate = 1.0 / math.sqrt(n_dp * rows)
    updated = call(
        functools.partial(update_body, per, sub, rate),
        jax.ShapeDtypeStruct((27, per, channels), F32),
        (ids, *owned, by_tap(momentum), by_tap(noise)), 2.0,
    )
    return jnp.swapaxes(updated, 0, 1)[None]


def solution(mesh):
    placed = (
        P("segment", "dp", None, None, None, None),
        P("segment", "dp", None, None, None, None),
        P("dp", None, None, None, None),
        P("segment", "dp", None, None),
        P("segment", "dp", None, None),
        P("segment", "dp", None, None),
    )

    def shards(activations, preacts, out_grad, weights, momentum, noise):
        channels = weights.shape[-1]
        n_dp = mesh.shape["dp"]
        fits = (
            mesh.shape["segment"] == 4
            and channels % (32 * n_dp) == 0
            and n_dp == 8
            and out_grad.shape[3] == 8
        )
        plan = quartered_shards if fits else general_shards
        return plan(activations, preacts, out_grad, weights, momentum, noise)

    return jax.shard_map(
        shards,
        mesh=mesh,
        in_specs=placed,
        out_specs=P("segment", "dp", None, None),
        check_vma=False,
    )
```

```python
import functools
import math

import jax
import jax.numpy as jnp
from jax import lax
from jax.experimental import pallas as pl
from jax.experimental.pallas import tpu as pltpu
from jax.sharding import PartitionSpec as P

BF16 = jnp.bfloat16
F32 = jnp.float32
VMEM_BYTES = 48 * 1024 * 1024
PEAK_PER_US = 1.1535e9
WEIGHT = 10


def shifted(x, axis, by):
    size = lax.axis_size(axis)
    pairs = [(i, i + by) for i in range(size) if 0 <= i + by < size]
    return lax.ppermute(x, axis, pairs)


def swapped(x, axis, mask):
    return lax.ppermute(x, axis, [(i, i ^ mask) for i in range(lax.axis_size(axis))])


def tap_stack(field, sign):
    batch_n, span_t, span_x, span_y, channels = field.shape
    padded = jnp.pad(field, ((0, 0), (1, 1), (1, 1), (1, 1), (0, 0)))
    views = []
    for along_t in (-1, 0, 1):
        for along_x in (-1, 0, 1):
            for along_y in (-1, 0, 1):
                start_t = 1 + sign * along_t
                start_x = 1 + sign * along_x
                start_y = 1 + sign * along_y
                views.append(
                    padded[
                        :,
                        start_t : start_t + span_t,
                        start_x : start_x + span_x,
                        start_y : start_y + span_y,
                        :,
                    ]
                )
    return jnp.stack(views, axis=4).reshape(batch_n * span_t * span_x * span_y, 27, channels)


def general_shards(activations, preacts, out_grad, weights, momentum, noise):
    segments = lax.axis_size("segment")
    devices_dp = lax.axis_size("dp")
    segment_id = lax.axis_index("segment")
    kernel = lax.all_gather(weights.astype(BF16), "dp", axis=1, tiled=True)[0]
    inputs = activations[0]
    pres = preacts[0]
    micro, span_t, span_x, span_y, channels = inputs.shape
    cells = span_t * span_x * span_y
    is_last = segment_id == segments - 1

    def step_fn(step, carry):
        incoming, total = carry
        index = step - (segments - 1 - segment_id)
        valid = jnp.logical_and(index >= 0, index < micro)
        clipped = jnp.clip(index, 0, micro - 1)
        given = lax.dynamic_index_in_dim(out_grad, clipped, 0, keepdims=False)
        upstream = jnp.where(is_last, given, incoming)
        pre = lax.dynamic_index_in_dim(pres, clipped, 0, keepdims=False).astype(F32)
        sig = jax.nn.sigmoid(pre)
        up_wide = upstream.astype(F32)
        grad_pre = (up_wide * sig * (1.0 + pre * (1.0 - sig)) * valid.astype(F32)).astype(BF16)
        pre_cols = tap_stack(grad_pre[None], -1)
        back = jnp.einsum("nto,cto->nc", pre_cols, kernel, preferred_element_type=F32)
        passed = (up_wide + back.reshape(upstream.shape)).astype(BF16)
        in_cols = tap_stack(lax.dynamic_index_in_dim(inputs, clipped, 0, keepdims=True), 1)
        total = total + jnp.einsum(
            "ntc,no->cto", in_cols, grad_pre.reshape(cells, channels), preferred_element_type=F32
        )
        return shifted(passed, "segment", -1), total

    init = (jnp.zeros(inputs.shape[1:], BF16), jnp.zeros((channels, 27, channels), F32))
    total = lax.fori_loop(0, micro + segments - 1, step_fn, init)[1]
    owned = lax.psum_scatter(total, "dp", scatter_dimension=0, tiled=True)
    rate = 1.0 / math.sqrt(devices_dp * micro * cells)
    return (0.9 * momentum[0] - rate * owned + 0.3 * noise[0])[None]


def iota(shape, dim):
    return lax.broadcasted_iota(jnp.int32, shape, dim)


def log2(n):
    return n.bit_length() - 1


def channel_of(place, quarter, per, sub):
    return (place >> log2(sub)) * per + quarter * sub + (place & (sub - 1))


def dot(a, b):
    return jnp.dot(a, b, preferred_element_type=F32)


def call(body, out_shape, args, us, scratch=()):
    return pl.pallas_call(
        body,
        out_shape=out_shape,
        in_specs=[pl.BlockSpec(memory_space=pltpu.SMEM)]
        + [pl.BlockSpec(memory_space=pltpu.VMEM)] * (len(args) - 1),
        out_specs=jax.tree.map(lambda _: pl.BlockSpec(memory_space=pltpu.VMEM), out_shape),
        scratch_shapes=list(scratch),
        compiler_params=pltpu.CompilerParams(vmem_limit_bytes=VMEM_BYTES),
        cost_estimate=pl.CostEstimate(
            flops=int(us * WEIGHT * PEAK_PER_US), bytes_accessed=0, transcendentals=0
        ),
    )(*args)


def weights_body(per, sub, ids, w_ref, *out_refs):
    channels = w_ref.shape[2]
    quarter_n = channels // 4
    s = ids[0]
    lane = iota((channels, channels), 1)
    place = lane & (quarter_n - 1)
    for m, out_ref in enumerate(out_refs):
        target = s ^ m
        own = w_ref[:, pl.ds(pl.multiple_of(target * sub, sub), sub), :]
        quarter = (lane >> log2(quarter_n)) ^ target
        order = iota((channels, channels), 0) == channel_of(place, quarter, per, sub)
        moved = dot(own.reshape(27 * sub, channels).astype(BF16), order.astype(BF16))
        for bc in range(9):
            part = [moved[(a * 9 + bc) * sub : (a * 9 + bc + 1) * sub] for a in range(3)]
            out_ref[:, bc * channels : (bc + 1) * channels] = jnp.concatenate(part, axis=0).astype(
                BF16
            )


def packing(channels, s, per, sub):
    quarter_n = channels // 4
    shape = (channels, 8 * quarter_n)
    lane = iota(shape, 1)
    place = lane & (quarter_n - 1)
    quarter = (lane >> log2(2 * quarter_n)) ^ s
    hit = iota(shape, 0) == channel_of(place, quarter, per, sub)
    low = (lane & (2 * quarter_n - 1)) < quarter_n
    first = jnp.logical_and(hit, low).astype(BF16)
    second = jnp.logical_and(hit, jnp.logical_not(low)).astype(BF16)
    return first, second


def packed_into(refs, field, first, second):
    half = field.shape[0] // 2
    width = first.shape[1] // 4
    lanes = width * len(refs)
    moved = dot(field[:half], first[:, :lanes]) + dot(field[half:], second[:, :lanes])
    for m, ref in enumerate(refs):
        ref[...] = moved[:, m * width : (m + 1) * width].astype(BF16)


def preacts_body(per, sub, ids, pre_ref, up_ref, up_out, *out_refs):
    first, second = packing(pre_ref.shape[1], ids[0], per, sub)
    packed_into(out_refs, pre_ref, first, second)
    packed_into([up_out], up_ref, first, second)


def first_body(per, sub, ids, up_ref, pre_ref, x_ref, *out_refs):
    half = up_ref.shape[0]
    packed_into([r.at[half:] for r in out_refs], x_ref, *packing(x_ref.shape[1], ids[0], per, sub))
    grad_pre = silu_back(up_ref[...].astype(F32), pre_ref[...])
    for ref in out_refs:
        ref[:half] = grad_pre


def silu_back(up_wide, pre):
    pre = pre.astype(F32)
    sig = jax.nn.sigmoid(pre)
    return (up_wide * sig * (1.0 + pre * (1.0 - sig))).astype(BF16)


def shifts(field, span):
    span_x, span_y = span
    rows, lanes = field.shape
    y = iota((rows, lanes), 0) & (span_y - 1)
    along_y = (
        jnp.where(y == span_y - 1, 0.0, pltpu.roll(field, rows - 1, 0)),
        field,
        jnp.where(y == 0, 0.0, pltpu.roll(field, 1, 0)),
    )
    out = []
    for b in (-1, 0, 1):
        for c in (-1, 0, 1):
            part = along_y[c + 1].reshape(rows // (span_x * span_y), span_x, span_y, lanes)
            edge = jnp.zeros_like(part[:, :1])
            if b == 1:
                part = jnp.concatenate([edge, part[:, :-1]], axis=1)
            elif b == -1:
                part = jnp.concatenate([part[:, 1:], edge], axis=1)
            out.append(part.reshape(rows, lanes))
    return out


def fill_columns(cols, parts, half, span):
    width = parts[0].shape[1]
    quarter_n = width // 2
    channels = 4 * quarter_n
    shape = (4 * width, 2 * channels)
    src, dst = iota(shape, 0), iota(shape, 1)
    m, h, place = src >> log2(width), (src >> log2(quarter_n)) & 1, src & (quarter_n - 1)
    unpack = (dst == h * channels + m * quarter_n + place).astype(BF16)
    both = dot(jnp.concatenate([part[:half] for part in parts], axis=1), unpack)
    field = jnp.concatenate([both[:, :channels], both[:, channels:]], axis=0)
    for k, part in enumerate(shifts(field, span[1:])):
        cols[:, k * channels : (k + 1) * channels] = part.astype(BF16)


def find_back(cols, w_ref, up_ref, pre_ref, up_out, g_out, span, n_dp, d):
    span_t, span_x, span_y = span
    half, width = up_ref.shape
    quarter_n = width // 2
    sub = quarter_n // n_dp
    rows = 2 * half
    plane = span_x * span_y
    shape = (3 * quarter_n, 3 * quarter_n)
    dst, src = iota(shape, 0), iota(shape, 1)
    a, place = dst >> log2(quarter_n), dst & (quarter_n - 1)
    apart = (place >> log2(sub)) ^ d
    piece = ((apart >> 2) & 1) + (apart & 2) + (n_dp // 2) * (apart & 1)
    order = src == piece * (3 * sub) + a * sub + (place & (sub - 1))
    kernel = dot(order.astype(BF16), w_ref[...]).astype(BF16)
    terms = lax.dot_general(
        cols[...], kernel, (((1,), (1,)), ((), ())), preferred_element_type=F32
    )
    back = []
    for a in range(3):
        back.append(
            terms[:, a * quarter_n : (a + 1) * quarter_n].reshape(
                rows // (span_t * plane), span_t, plane, quarter_n
            )
        )
    edge = jnp.zeros_like(back[0][:, :1])
    total = (
        back[1]
        + jnp.concatenate([back[0][:, 1:], edge], axis=1)
        + jnp.concatenate([edge, back[2][:, :-1]], axis=1)
    ).reshape(rows, quarter_n)
    total = jnp.concatenate([total[:half], total[half:]], axis=1)
    passed = (up_ref[...].astype(F32) + total).astype(BF16)
    up_out[...] = passed
    g_out[...] = silu_back(passed.astype(F32), pre_ref[...])


def find_terms(cols, x_ref, keep, give, total, span, n_dp, d):
    span_t, span_x, span_y = span
    half, width = x_ref.shape
    quarter_n = width // 2
    sub = quarter_n // n_dp
    plane = span_x * span_y
    shape = (width, 2 * width)
    src, dst = iota(shape, 0), iota(shape, 1)
    twice = jnp.logical_and(
        (src & (quarter_n - 1)) == (dst & (quarter_n - 1)),
        (src >> log2(quarter_n)) == (dst >> log2(width)),
    ).astype(BF16)
    both = dot(x_ref[...], twice)
    field = jnp.concatenate([both[:, :width], both[:, width:]], axis=0)
    field = field.reshape(2 * half // (span_t * plane), span_t, plane, width)
    edge = jnp.zeros_like(field[:, :1])
    later = jnp.concatenate([field[:, 1:], edge], axis=1)
    earlier = jnp.concatenate([edge, field[:, :-1]], axis=1)
    left = iota(field.shape, 3) < quarter_n
    taps = jnp.concatenate([jnp.where(left, earlier, field), later], axis=3)
    taps = taps.reshape(2 * half, 2 * width)[:, : 3 * quarter_n].astype(BF16)
    total[...] = lax.dot_general(
        taps, cols[...], (((0,), (0,)), ((), ())), preferred_element_type=F32
    )
    for k in range(n_dp // 2):
        for bit, ref in ((0, keep), (1, give)):
            owner = d ^ (2 * k + bit)
            own = [
                total[pl.ds(pl.multiple_of(a * quarter_n + owner * sub, sub), sub), :]
                for a in range(3)
            ]
            ref[k] = jnp.concatenate(own, axis=0).astype(ref.dtype)


def back_body(span, n_dp, ids, g0, g1, g2, g3, w_ref, up_ref, pre_ref, up_out, g_out, cols):
    fill_columns(cols, (g0, g1, g2, g3), up_ref.shape[0], span)
    find_back(cols, w_ref, up_ref, pre_ref, up_out, g_out, span, n_dp, ids[1])


def section_body(
    span, n_dp, ids, g0, g1, g2, g3, w_ref, up_ref, pre_ref, x_ref, up_out, g_out, keep, give, cols, total
):
    fill_columns(cols, (g0, g1, g2, g3), up_ref.shape[0], span)
    find_back(cols, w_ref, up_ref, pre_ref, up_out, g_out, span, n_dp, ids[1])
    find_terms(cols, x_ref, keep, give, total, span, n_dp, ids[1])


def terms_body(span, n_dp, ids, g0, g1, g2, g3, x_ref, keep, give, cols, total):
    fill_columns(cols, (g0, g1, g2, g3), x_ref.shape[0], span)
    find_terms(cols, x_ref, keep, give, total, span, n_dp, ids[1])


def pair_body(ids, keep, other, stay, send):
    for k in range(keep.shape[0]):
        total = keep[k] + other[k].astype(F32)
        if k % 2 == 0:
            stay[k // 2] = total
        else:
            send[k // 2] = total.astype(BF16)


def next_body(ids, stay, other, own, send):
    own[...] = stay[0] + other[0].astype(F32)
    send[...] = (stay[1] + other[1].astype(F32)).astype(BF16)


def sums_body(ids, *refs):
    ins, outs = refs[:8], refs[8:]
    s = ids[0]
    for section in range(4):
        total = (ins[2 * section][...] + ins[2 * section + 1][...].astype(F32)).astype(BF16)
        for m, out_ref in enumerate(outs):
            @pl.when((s ^ m) == section)
            def _(out_ref=out_ref, total=total):
                out_ref[...] = total


def update_body(per, sub, rate, ids, f0, f1, f2, f3, momentum, noise, out):
    channels = momentum.shape[2]
    quarter_n = channels // 4
    s = ids[0]
    lane = iota((channels, channels), 0)
    for m, f in enumerate((f0, f1, f2, f3)):
        source = s ^ m
        place, quarter = lane & (quarter_n - 1), (lane >> log2(quarter_n)) ^ source
        order = iota((channels, channels), 1) == channel_of(place, quarter, per, sub)
        wide = f[...].astype(F32)
        parts = [
            wide[a * sub : (a + 1) * sub, bc * channels : (bc + 1) * channels]
            for a in range(3)
            for bc in range(9)
        ]
        grads = dot(jnp.concatenate(parts, axis=0).astype(BF16), order.astype(BF16))
        rows = pl.ds(pl.multiple_of(source * sub, sub), sub)
        out[:, rows, :] = (
            0.9 * momentum[:, rows, :]
            - rate * grads.reshape(27, sub, channels)
            + 0.3 * noise[:, rows, :]
        )


def pick(index, arrays):
    return lax.select_n(index, *arrays)


def after(x, *others):
    return lax.optimization_barrier((x, *others))[0]


def quartered_shards(activations, preacts, out_grad, weights, momentum, noise):
    n_dp = lax.axis_size("dp")
    s = lax.axis_index("segment").astype(jnp.int32)
    d = lax.axis_index("dp").astype(jnp.int32)
    ids = jnp.stack([s, d])
    micro, span_t, span_x, span_y, channels = out_grad.shape
    span = (span_t, span_x, span_y)
    rows = micro * span_t * span_x * span_y
    quarter_n = channels // 4
    width = 2 * quarter_n
    half = rows // 2
    per = channels // n_dp
    sub = per // 4
    inputs = activations.reshape(rows, channels)
    pres = preacts.reshape(rows, channels)
    packed = jax.ShapeDtypeStruct((half, width), BF16)
    piece = (3 * sub, 9 * channels)
    columns = pltpu.VMEM((rows, 9 * channels), BF16)

    def array(dtype, *lead):
        return jax.ShapeDtypeStruct(lead + piece, dtype)

    def by_tap(x):
        return jnp.swapaxes(x[0], 0, 1)

    def spread(parts):
        far, one, two = (swapped(parts[m], "segment", m) for m in (3, 1, 2))
        return parts[0], one, two, far

    w_held = spread(
        call(functools.partial(weights_body, per, sub), [array(BF16)] * 4, (ids, by_tap(weights)), 0.9)
    )
    up, *p_parts = call(
        functools.partial(preacts_body, per, sub),
        [packed] * 5,
        (ids, pres, out_grad.reshape(rows, channels)), 1.1,
    )
    p_held = spread(p_parts)

    def far_half(own, *others):
        return jnp.stack([own, after(swapped(own, "dp", 4), *others)])

    def all_chips(pieces, *others):
        return jnp.concatenate([pieces, after(swapped(pieces, "dp", 2), *others)], axis=0)

    def both_cores(pieces):
        other = swapped(pieces, "dp", 1)
        return jnp.concatenate([pieces, other], axis=0).reshape(3 * quarter_n, 9 * channels)

    def terms(field, x):
        return call(
            functools.partial(terms_body, span, n_dp),
            [array(F32, 4), array(BF16, 4)],
            (ids, *field, x), 2.6,
            scratch=[columns, pltpu.VMEM((3 * quarter_n, 9 * channels), F32)],
        )

    def paired(keep, give):
        return call(
            pair_body, [array(F32, 2), array(BF16, 2)], (ids, keep, swapped(give, "dp", 1)), 0.6
        )

    def reduced(stay, send, *others):
        other = after(swapped(send, "dp", 2), *others)
        return call(next_body, [array(F32), array(BF16)], (ids, stay, other), 0.6)

    def summed(own, send):
        return own, swapped(send, "dp", 4)

    def back(section, field, up):
        return call(
            functools.partial(back_body, span, n_dp),
            [packed] * 2,
            (ids, *field, kernels[section], up, pick(s ^ (section - 1), p_held)), 3.0,
            scratch=[columns],
        )

    def back_and_terms(section, field, up):
        up, g, *terms = call(
            functools.partial(section_body, span, n_dp),
            [packed, packed, array(F32, 4), array(BF16, 4)],
            (
                ids, *field, kernels[section], up,
                pick(s ^ (section - 1), p_held), pick(s ^ section, x_held),
            ), 3.8,
            scratch=[columns, pltpu.VMEM((3 * quarter_n, 9 * channels), F32)],
        )
        return up, g, terms

    def tied(field, *others):
        return lax.optimization_barrier((tuple(field), others))[0]

    def tied(field, *others):
        return lax.optimization_barrier((tuple(field), others))[0]

    kernels = {}
    first = call(
        functools.partial(first_body, per, sub),
        [jax.ShapeDtypeStruct((rows, width), BF16)] * 4,
        (ids, up, pick(s ^ 3, p_held), inputs), 1.1,
    )
    field3 = spread(first)
    half3 = far_half(after(pick(s ^ 3, w_held), *p_parts))
    chips3 = all_chips(after(half3, first[0]))
    kernels[3] = both_cores(chips3)
    x_held = [x[half:] for x in field3]
    half2 = far_half(after(pick(s ^ 2, w_held), half3, first[0]))
    up, g2 = back(3, field3, up)
    field2 = spread([g2] * 4)
    chips2 = all_chips(half2, g2)
    kernels[2] = both_cores(chips2)
    half1 = far_half(after(pick(s ^ 1, w_held), chips3), g2)
    terms3 = terms(tied(field3, g2), pick(s ^ 3, x_held))
    up, g1, terms2 = back_and_terms(2, tied(field2, terms3), up)
    field1 = spread([g1] * 4)
    chips1 = all_chips(half1, g1)
    kernels[1] = both_cores(chips1)
    terms3 = paired(*tied(terms3, g1))
    terms2 = paired(*terms2)
    up, g0, terms1 = back_and_terms(1, tied(field1, terms2, terms3), up)
    field0 = spread([g0] * 4)
    terms1 = paired(*terms1)
    terms0 = terms(tied(field0, terms1), pick(s, x_held))
    terms3 = reduced(*terms3, terms0[0])
    terms0 = paired(*terms0)
    sum3 = summed(*terms3)
    terms2 = reduced(*terms2)
    terms1 = reduced(*terms1, terms0)
    terms0 = reduced(*terms0)
    sums = [summed(*terms0), summed(*terms1), summed(*terms2), sum3]
    owned = spread(
        call(sums_body, [array(BF16)] * 4, (ids, *sums[0], *sums[1], *sums[2], *sums[3]), 0.7)
    )
    rate = 1.0 / math.sqrt(n_dp * rows)
    updated = call(
        functools.partial(update_body, per, sub, rate),
        jax.ShapeDtypeStruct((27, per, channels), F32),
        (ids, *owned, by_tap(momentum), by_tap(noise)), 2.0,
    )
    return jnp.swapaxes(updated, 0, 1)[None]


def solution(mesh):
    placed = (
        P("segment", "dp", None, None, None, None),
        P("segment", "dp", None, None, None, None),
        P("dp", None, None, None, None),
        P("segment", "dp", None, None),
        P("segment", "dp", None, None),
        P("segment", "dp", None, None),
    )

    def shards(activations, preacts, out_grad, weights, momentum, noise):
        channels = weights.shape[-1]
        n_dp = mesh.shape["dp"]
        fits = (
            mesh.shape["segment"] == 4
            and channels % (32 * n_dp) == 0
            and n_dp == 8
            and out_grad.shape[3] == 8
        )
        plan = quartered_shards if fits else general_shards
        return plan(activations, preacts, out_grad, weights, momentum, noise)

    return jax.shard_map(
        shards,
        mesh=mesh,
        in_specs=placed,
        out_specs=P("segment", "dp", None, None),
        check_vma=False,
    )
```
